128 devices in a mesh: row: 16 (over y, x_lo, core), col: 8 (over x_hi, z).
Axes of the slice: x: 4 (x_hi: 2, x_lo: 2; x = x_hi * 2 + x_lo), y: 4, z: 4, core: 2. Of those that a mesh axis runs over, the one named last changes fastest.
Arguments:
- features: bfloat16 [65536, 256], P(('row', 'col')), may hold values from -6 to 6
- weight: bfloat16 [256, 256], replicated, may hold values from -0.375 to 0.375
- bias: float32 [256], replicated, may hold values from -3 to 3
- tile_values: bfloat16 [16, 8, 448, 128, 128], P('row', 'col'), may hold values from -0.09375 to 0.09375
- tile_index: int32 [16, 8, 448, 2], P('row', 'col'), may hold values from 0 to 63, as said below
- tile_count: int32 [16, 8], P('row', 'col'), may hold values from 1 to 448
- out_grad: bfloat16 [65536, 256], P(('row', 'col')), may hold values from -6 to 6
Outputs:
- output: bfloat16 [65536, 256], P(('row', 'col'))
- feat_grad: bfloat16 [65536, 256], P(('row', 'col'))
- weight_grad: float32 [256, 256], replicated
- bias_grad: float32 [256], replicated
The draws below stay inside these ranges and needn't reach their ends.
Inputs may be any that keep to these rules, and one draw needn't show every extreme that they name: `tile_index`: column k is a row tile (below 32) for k = 0 and a column tile for k = 1; the slots of one cell name distinct tile positions.
All inputs are finite; a program needn't handle non-finite values.
Results may differ from the reference program's by a relative error of at most 0.007.
Values may be sent and summed in bfloat16 or wider, within the bound.
A program may use at most 128 MiB of HBM per device.

```python
import jax
import jax.numpy as jnp
from jax import lax

FEAT_IN = 256
FEAT_OUT = 256
TILE = 128
ROWS_DEV = 512
NODES = 65536
ROWBLK = 4096
COLBLK = 8192
TILES = 448
N_ROW = 16
N_COL = 8


def draw_tile_index(key, part):
    key = jax.random.fold_in(key, 11)
    row_tiles = ROWS_DEV * N_COL // TILE
    col_tiles = ROWS_DEV * N_ROW // TILE
    slots = row_tiles * col_tiles
    last_slot = slots - 1

    def cell(number):
        order = jax.random.permutation(jax.random.fold_in(key, number), slots).astype(jnp.int32)
        where_last = jnp.argmax(order == last_slot)
        forced = order.at[where_last].set(order[0]).at[0].set(last_slot)
        order = jnp.where(number == 0, forced, order)
        picked = order[:TILES]
        return jnp.stack([picked // col_tiles, picked % col_tiles], axis=1).astype(jnp.int32)
    cells = jax.vmap(cell)(jnp.arange(N_ROW * N_COL, dtype=jnp.int32))
    return cells.reshape(N_ROW, N_COL, TILES, 2)


def draw_tile_count(key, part):
    key = jax.random.fold_in(key, 23)
    counts = jax.random.randint(key, (N_ROW * N_COL,), max(1, TILES // 8), TILES // 2 + 1).astype(jnp.int32)
    busiest = jax.random.randint(jax.random.fold_in(key, 1), (), 0, N_ROW * N_COL)
    counts = counts.at[busiest].set(TILES)
    return counts.reshape(N_ROW, N_COL).astype(jnp.int32)


def levels(own_key, extent, shards, low, largest):
    def one(position, parts):
        draws = jax.random.uniform(jax.random.fold_in(jax.random.fold_in(own_key, 6), position), (parts,), jnp.float32, low / len(shards), largest / len(shards))
        return jnp.repeat(jnp.exp(draws), extent[position] // parts).reshape((-1,) + (1,) * (len(extent) - position - 1))

    loudness = one(*shards[0])
    for cut in shards[1:]:
        loudness = loudness * one(*cut)
    return loudness


def normal_values(stream_key, extent, scale, most, shards=(), kind=jnp.bfloat16):
    result = scale * jax.random.normal(stream_key, extent, jnp.float32)
    if shards:
        result = result * levels(stream_key, extent, shards, -0.22, 0.18)
    return jnp.clip(result, -most, most).astype(kind)


def setup_inputs(seed: int = 0) -> dict:
    keys = jax.random.split(jax.random.key(seed), 8)
    return {
        "features": normal_values(keys[0], (NODES, FEAT_IN), 1.0, 6.0, ((0, 128),)),
        "weight": normal_values(keys[1], (FEAT_IN, FEAT_OUT), FEAT_IN ** -0.5, 0.375),
        "bias": normal_values(keys[2], (FEAT_OUT,), 0.5, 3.0, (), jnp.float32),
        "tile_values": normal_values(keys[3], (N_ROW, N_COL, TILES, TILE, TILE), (N_COL * TILES * TILE * TILE // (3 * ROWBLK)) ** -0.5, 0.09375, ((0, 16), (1, 8))),
        "tile_index": draw_tile_index(jax.random.fold_in(keys[7], 71), 0),
        "tile_count": draw_tile_count(jax.random.fold_in(keys[7], 71), 0),
        "out_grad": normal_values(keys[6], (NODES, FEAT_OUT), 1.0, 6.0, ((0, 128),)),
    }


def spread(values, target, source_idx, live, source, target_tiles, flip):
    width = source.shape[1]
    tile = values.shape[1]
    count = values.shape[0]
    blocks = source.reshape(-1, tile, width)
    step = min(64, count)
    turns = count // step

    def one(acc, number):
        start = number * step
        vals = lax.dynamic_slice_in_dim(values, start, step, 0).astype(jnp.float32)
        dest = lax.dynamic_slice_in_dim(target, start, step, 0)
        anchor = lax.dynamic_slice_in_dim(source_idx, start, step, 0)
        alive = lax.dynamic_slice_in_dim(live, start, step, 0)
        picked = blocks[anchor].astype(jnp.float32)
        if flip:
            product = jnp.einsum("tab,taf->tbf", vals, picked)
        else:
            product = jnp.einsum("tab,tbf->taf", vals, picked)
        product = jnp.where(alive[:, None, None], product, jnp.zeros_like(product))
        acc = acc.at[dest].add(product)
        return acc, None

    start_acc = jnp.zeros((target_tiles, tile, width), jnp.float32)
    acc, _ = lax.scan(one, start_acc, jnp.arange(turns, dtype=jnp.int32))
    return acc.reshape(target_tiles * tile, width)


def reference(features, weight, bias, tile_values, tile_index, tile_count, out_grad):
    nodes = features.shape[0]
    fout = weight.shape[1]
    projected = jnp.dot(features, weight, preferred_element_type=jnp.float32).astype(jnp.bfloat16)
    column_src = projected.reshape(N_ROW, N_COL, ROWS_DEV, fout).transpose(1, 0, 2, 3).reshape(N_COL, COLBLK, fout)
    live = jnp.arange(TILES, dtype=jnp.int32)[None, None, :] < tile_count[:, :, None]

    def row_block(i):
        def cell(acc, j):
            part = spread(tile_values[i, j], tile_index[i, j, :, 0], tile_index[i, j, :, 1], live[i, j], column_src[j], ROWBLK // TILE, False)
            return acc + part, None
        acc, _ = lax.scan(cell, jnp.zeros((ROWBLK, fout), jnp.float32), jnp.arange(N_COL, dtype=jnp.int32))
        return acc

    aggregated = lax.map(row_block, jnp.arange(N_ROW, dtype=jnp.int32)).reshape(nodes, fout)
    pre = aggregated + bias
    sig = jax.nn.sigmoid(pre)
    output = (pre * sig).astype(jnp.bfloat16)
    slope = sig * (1.0 + pre * (1.0 - sig))
    pre_grad = (out_grad.astype(jnp.float32) * slope).astype(jnp.bfloat16)
    bias_grad = jnp.sum(pre_grad.astype(jnp.float32), axis=0)
    grad_rows = pre_grad.reshape(N_ROW, ROWBLK, fout)

    def col_block(j):
        def cell(acc, i):
            part = spread(tile_values[i, j], tile_index[i, j, :, 1], tile_index[i, j, :, 0], live[i, j], grad_rows[i], COLBLK // TILE, True)
            return acc + part, None
        acc, _ = lax.scan(cell, jnp.zeros((COLBLK, fout), jnp.float32), jnp.arange(N_ROW, dtype=jnp.int32))
        return acc

    back_cols = lax.map(col_block, jnp.arange(N_COL, dtype=jnp.int32))
    back = back_cols.reshape(N_COL, N_ROW, ROWS_DEV, fout).transpose(1, 0, 2, 3).reshape(nodes, fout)
    back_b = back.astype(jnp.bfloat16)
    feat_grad = jnp.dot(back_b, weight.T, preferred_element_type=jnp.float32).astype(jnp.bfloat16)
    weight_grad = jnp.dot(features.T, back_b, preferred_element_type=jnp.float32)
    return output, feat_grad, weight_grad, bias_grad
```

```python
import functools

import jax
import jax.numpy as jnp
from jax import lax
from jax.experimental import pallas as pl
from jax.experimental.pallas import tpu as pltpu
from jax.sharding import PartitionSpec as P

MESH = pl.DeviceIdType.MESH
TILE = 128
BLK = 4
SLOTS = 448
NR, NC = 32, 64
FPAIRS, BPAIRS = 240, 256
ZERO_RUN = 256
UNROLL = 4
F32, BF16, I32 = jnp.float32, jnp.bfloat16, jnp.int32


def pair_lists(dst_r, dst_c, src_c, live_r, live_c, nd, ns):
    t_r = lax.broadcasted_iota(I32, (SLOTS, SLOTS), 1)
    t_c = lax.broadcasted_iota(I32, (SLOTS, SLOTS), 0)
    one = lambda m: m.astype(I32)
    dlive_r = jnp.where(live_r, dst_r, nd)
    dlive_c = jnp.where(live_c, dst_c, nd)
    own_cn = dlive_c == lax.broadcasted_iota(I32, (SLOTS, nd), 1)
    own_nr = dlive_r == lax.broadcasted_iota(I32, (nd, SLOTS), 0)
    n_r = jnp.sum(one(own_cn), axis=0, keepdims=True)
    n_c = jnp.sum(one(own_nr), axis=1, keepdims=True)
    half_c = (n_c + 1) // 2
    half_r = (n_r + 1) // 2
    g_c = lax.broadcasted_iota(I32, (nd, nd), 0)
    g_r = lax.broadcasted_iota(I32, (nd, nd), 1)
    base_r = jnp.sum(jnp.where(g_c < g_r, half_c, 0), axis=0, keepdims=True)
    base_c = jnp.sum(jnp.where(g_r < g_c, half_r, 0), axis=1, keepdims=True)
    rank_c = jnp.sum(one((dlive_c == dlive_r) & (t_r < t_c)), axis=1, keepdims=True)
    pos_c = jnp.sum(jnp.where(own_cn, 2 * base_r, 0), axis=1, keepdims=True) + rank_c
    pos_c = jnp.where(live_c, pos_c, 4096)
    hit = pos_c == lax.broadcasted_iota(I32, (SLOTS, 512), 1)
    slot = lax.broadcasted_iota(I32, (SLOTS, 512), 0)
    tile_l = jnp.sum(jnp.where(hit, slot, 0), axis=0, keepdims=True)
    src_l = jnp.sum(jnp.where(hit, src_c - ns, 0), axis=0, keepdims=True) + ns
    first = (base_c == lax.broadcasted_iota(I32, (nd, 512), 1)) & (n_c > 0)
    keep_l = 1 - jnp.sum(one(first), axis=0, keepdims=True)
    end_r = jnp.where(n_r > 0, base_r + half_r - 1, ZERO_RUN)
    return tile_l, src_l, keep_l, end_r


def kernel(H, feat, weight, bias, tiles_hbm, idx_c, idx_r, cnt, ograd,
           output, fgrad, dw_out, db_out,
           tiles, runs, lists_v, lists, xs, ps, gs, qs, sib, rsa, rsb, rsa2, rsb2, sa, sb, ybf, zb,
           dbuf, drs, dp, dq, dfin, ss, rs, ls):
    w = 256 // H
    i, j = lax.axis_index("row"), lax.axis_index("col")
    y, xl, c = i // 4, lax.rem(i // 2, 2), lax.rem(i, 2)
    xh, z = j // 4, lax.rem(j, 4)
    m4 = lambda v: lax.rem(v + 4, 4)

    class Row:
        p, q = y, xl
        slot = staticmethod(lambda p, q: (p * 2 + q) * 2 + c)
        dev = staticmethod(lambda p, q: ((p * 2 + q) * 2 + c, j))

    class Col:
        p, q = z, xh
        slot = staticmethod(lambda p, q: q * 4 + p)
        dev = staticmethod(lambda p, q: (i, q * 4 + p))

    sibling = ((y * 2 + xl) * 2 + 1 - c, j)
    peers = [lax.rem(i + d, 16) for d in range(1, 16)]
    cpeers = [lax.rem(j + d, 8) for d in range(1, 8)]

    sent = []

    def send(src, dst, dev):
        n = len(sent)
        cp = pltpu.make_async_remote_copy(src_ref=src, dst_ref=dst, send_sem=ss.at[n], recv_sem=rs.at[n],
                                          device_id=dev, device_id_type=MESH)
        cp.start()
        sent.append(cp)
        return cp

    load_tiles = pltpu.make_async_copy(tiles_hbm.at[0, 0], tiles, ls.at[0])
    load_tiles.start()
    loads = []
    for h in range(H):
        for t in range(BLK):
            cp = pltpu.make_async_copy(feat.at[pl.ds(t * TILE, TILE), pl.ds(h * w, w)], xs[h].at[i * BLK + t],
                                       ls.at[1 + h * BLK + t])
            cp.start()
            loads.append(cp)

    barrier = pltpu.get_barrier_semaphore()
    for r in peers:
        pl.semaphore_signal(barrier, inc=1, device_id=(r, j), device_id_type=MESH)
    for k in cpeers:
        pl.semaphore_signal(barrier, inc=1, device_id=(i, k), device_id_type=MESH)
    pl.semaphore_wait(barrier, 22)
    for cp in loads:
        cp.wait()

    blk = lambda buf, s, lo=0, n=BLK: buf.at[pl.ds(s * BLK + lo, n)]

    def gather(g, buf, relay):
        p, q = g.p, g.q
        own = blk(buf, g.slot(p, q))
        down = []
        cx = send(own, own, g.dev(p, 1 - q))
        cy = {d: send(own, own, g.dev(m4(p + d), q)) for d in (1, 3, 2)}
        if relay:
            down.append(send(own, own, sibling))
        yield
        cx.wait_recv()
        s = g.slot(p, 1 - q)
        part = blk(buf, s, 2, 2)
        cb = {d: send(part, part, g.dev(m4(p + d), q)) for d in (1, 3, 2)}
        if relay:
            down.append(send(blk(buf, s), blk(buf, s), sibling))
        ca = {}
        for d in (1, 3, 2):
            cy[d].wait_recv()
            s = g.slot(m4(p - d), q)
            part = blk(buf, s, 0, 2)
            ca[d] = send(part, part, g.dev(p, 1 - q))
            if relay:
                down.append(send(blk(buf, s), blk(buf, s), sibling))
        yield
        for d in (1, 3, 2):
            cb[d].wait_recv()
            ca[d].wait_recv()
            if relay:
                s = g.slot(m4(p - d), 1 - q)
                down.append(send(blk(buf, s), blk(buf, s), sibling))
        for cp in down:
            cp.wait_recv()

    def scatter(g, buf, k, h, emit):
        p, q = g.p, g.q
        ra, rb, ra2, rb2, oa, ob = rsa[k][h], rsb[k][h], rsa2[k][h], rsb2[k][h], sa[k][h], sb[k][h]
        xa, yb = {}, {}
        for d in (1, 3, 2, 0):
            xa[d] = send(blk(buf, g.slot(m4(p + d), 1 - q), 0, 2), ra.at[pl.ds(2 * d, 2)], g.dev(p, 1 - q))
        for d in (1, 3, 2):
            for e in (1, 0):
                qq = 1 - q if e else q
                yb[d, e] = send(blk(buf, g.slot(m4(p + d), qq), 2, 2), rb.at[pl.ds((d - 1) * 4 + e * 2, 2)],
                                g.dev(m4(p + d), q))
        yield
        y2 = {}
        for d in (1, 3, 2):
            xa[d].wait_recv()
            for t in range(2):
                own = buf[g.slot(m4(p + d), q) * BLK + t].astype(F32)
                oa[2 * d + t] = (own + ra[2 * d + t].astype(F32)).astype(BF16)
            y2[d] = send(oa.at[pl.ds(2 * d, 2)], ra2.at[pl.ds(2 * (d - 1), 2)], g.dev(m4(p + d), q))
        for d in (1, 3, 2):
            yb[d, 1].wait_recv()
        for t in range(2):
            tot = buf[g.slot(p, 1 - q) * BLK + 2 + t].astype(F32)
            for d in (1, 3, 2):
                tot = tot + rb[(d - 1) * 4 + 2 + t].astype(F32)
            ob[t] = tot.astype(BF16)
        x2 = send(ob, rb2, g.dev(p, 1 - q))
        yield
        xa[0].wait_recv()
        for d in (1, 3, 2):
            y2[d].wait_recv()
            yb[d, 0].wait_recv()
        for t in range(2):
            tot = buf[g.slot(p, q) * BLK + t].astype(F32) + ra[t].astype(F32)
            for d in (1, 3, 2):
                tot = tot + ra2[2 * (d - 1) + t].astype(F32)
            emit(t, tot)
        x2.wait_recv()
        for t in range(2):
            tot = buf[g.slot(p, q) * BLK + 2 + t].astype(F32)
            for d in (1, 3, 2):
                tot = tot + rb[(d - 1) * 4 + t].astype(F32)
            emit(2 + t, tot + rb2[t].astype(F32))

    def spmm(row, pairs, src, flip):
        dims = (((0,), (0,)), ((), ())) if flip else (((1,), (0,)), ((), ()))

        def body(n, acc):
            for u in range(UNROLL):
                k = n * UNROLL + u
                prod = lax.dot_general(tiles[lists[row, 2 * k]], src[lists[row + 1, 2 * k]], dims,
                                       preferred_element_type=F32)
                prod += lax.dot_general(tiles[lists[row, 2 * k + 1]], src[lists[row + 1, 2 * k + 1]], dims,
                                        preferred_element_type=F32)
                acc = acc * lists[row + 2, k].astype(F32) + prod
                runs[k] = acc.astype(BF16)
            return acc

        lax.fori_loop(0, pairs // UNROLL, body, jnp.zeros((TILE, w), F32))

    def collect(row, nd, dst):
        def body(r, _):
            dst[r] = runs[lists[row + 3, r]]
            return 0

        lax.fori_loop(0, nd, body, 0)

    def finish(gen):
        for _ in gen:
            pass

    ag = [gather(Row, xs[h], True) for h in range(H)]
    for g in ag:
        next(g)

    live_r = lax.broadcasted_iota(I32, (1, SLOTS), 1) < cnt[0, 0]
    live_c = lax.broadcasted_iota(I32, (SLOTS, 1), 0) < cnt[0, 0]
    r_r, c_r = idx_r[0:1, :], idx_r[1:2, :]
    r_c, c_c = idx_c[:, 0:1], idx_c[:, 1:2]
    lists_v[...] = jnp.zeros_like(lists_v)
    for row, (a, b, cc, nd, ns) in ((0, (r_r, r_c, c_c, NR, NC)), (4, (c_r, c_c, r_c, NC, NR))):
        t_l, s_l, k_l, e_l = pair_lists(a, b, cc, live_r, live_c, nd, ns)
        lists_v[row:row + 1, :] = t_l
        lists_v[row + 1:row + 2, :] = s_l
        lists_v[row + 2:row + 3, :] = k_l
        lists_v[row + 3:row + 4, 0:nd] = e_l
    cp = pltpu.make_async_copy(lists_v, lists, ls.at[1 + H * BLK])
    cp.start()
    runs[ZERO_RUN] = jnp.zeros((TILE, w), BF16)
    for h in range(H):
        xs[h][NC] = jnp.zeros((TILE, w), BF16)
        gs[h][NR] = jnp.zeros((TILE, w), BF16)
    cp.wait()
    load_tiles.wait()

    def put_y(h):
        def emit(t, v):
            ybf[pl.ds(t * TILE, TILE), pl.ds(h * w, w)] = v.astype(BF16)
        return emit

    sc = []
    for h in range(H):
        finish(ag[h])
        spmm(0, FPAIRS, xs[h], False)
        collect(0, NR, ps[h])
        g = scatter(Col, ps[h], 0, h, put_y(h))
        next(g)
        sc.append(g)
    for g in sc:
        finish(g)

    wb = weight[...]
    bsum = jnp.zeros((1, 256), F32)
    for t in range(BLK):
        rows = pl.ds(t * TILE, TILE)
        pre = jnp.dot(ybf[rows, :], wb, preferred_element_type=F32) + bias[...]
        sig = 1.0 / (1.0 + jnp.exp(-pre))
        output[rows, :] = (pre * sig).astype(BF16)
        slope = sig * (1.0 + pre * (1.0 - sig))
        pg = (ograd[rows, :].astype(F32) * slope).astype(BF16)
        bsum = bsum + jnp.sum(pg.astype(F32), axis=0, keepdims=True)
        zb[rows, :] = pg
        gw = lax.dot_general(pg, wb, (((1,), (1,)), ((), ())), preferred_element_type=F32).astype(BF16)
        for h in range(H):
            gs[h][j * BLK + t] = gw[:, h * w:(h + 1) * w]
    agc = [gather(Col, gs[h], False) for h in range(H)]
    for g in agc:
        next(g)

    dw = lax.dot_general(ybf[...], zb[...], (((0,), (0,)), ((), ())), preferred_element_type=F32)
    for k in range(8):
        dbuf[k, 0:32, :] = dw[k * 32:(k + 1) * 32, :]
        dbuf[k, 32:40, :] = jnp.broadcast_to(bsum, (8, 256))
    s1 = [send(dbuf.at[lax.rem(j + d, 8)], drs.at[j], (i, lax.rem(j + d, 8))) for d in range(1, 8)]
    drs[j] = dbuf[j]

    for h in range(H):
        next(agc[h])

    for cp in s1:
        cp.wait_recv()
    tot = drs[0]
    for k in range(1, 8):
        tot = tot + drs[k]
    me4 = xl * 2 + c
    dp[me4] = tot
    s2 = []
    for d in range(1, 4):
        o = lax.rem(me4 + d, 4)
        s2.append(send(dp.at[me4], dp.at[me4], (y * 4 + o, j)))

    def grad_2():
        for cp in s2:
            cp.wait_recv()
        dq[y] = (dp[0] + dp[1]) + (dp[2] + dp[3])
        return [send(dq.at[y], dq.at[y], (m4(y + d) * 4 + me4, j)) for d in (1, 3, 2)]

    def grad_3(s3):
        for cp in s3:
            cp.wait_recv()
        dfin[j] = (dq[0] + dq[1]) + (dq[2] + dq[3])
        return [send(dfin.at[j], dfin.at[j], (i, lax.rem(j + d, 8))) for d in range(1, 8)]

    def put_f(h):
        def emit(t, v):
            fgrad[pl.ds(t * TILE, TILE), pl.ds(h * w, w)] = v.astype(BF16)
        return emit

    late = None
    back = []
    for h in range(H):
        finish(agc[h])
        if h == 0:
            s3 = grad_2()
        spmm(4, BPAIRS, gs[h], True)
        collect(4, NC, qs[h])
        if h == 0:
            s4 = grad_3(s3)
        cps = {}
        for k in range(8):
            s = k * 2 + 1 - c
            cps[k] = send(blk(qs[h], s), sib[h].at[pl.ds(k * BLK, BLK)], sibling)
        for k in range(8):
            cps[k].wait_recv()
            for t in range(BLK):
                at = (k * 2 + c) * BLK + t
                qs[h][at] = (qs[h][at].astype(F32) + sib[h][k * BLK + t].astype(F32)).astype(BF16)
        g = scatter(Row, qs[h], 1, h, put_f(h))
        next(g)
        back.append(g)
    for cp in s4:
        cp.wait_recv()
    for k in range(8):
        dw_out[k * 32:(k + 1) * 32, :] = dfin[k, 0:32, :]
    db_out[...] = dfin[0, 32:33, :]
    for g in back:
        finish(g)
    for cp in sent:
        cp.wait_send()


def shards(H, features, weight, bias, tile_values, tile_index, tile_count, out_grad):
    w = 256 // H
    vm = lambda *s, dt=BF16: pltpu.VMEM(s, dt)
    many = lambda n, *s: [vm(n, *s)] * H
    blkT = (TILE, w)
    two = lambda n: [many(n, *blkT) for _ in range(2)]
    index = tile_index[0, 0]
    sems = 180
    scratch = [
        vm(SLOTS, TILE, TILE),
        vm(ZERO_RUN + 1, *blkT),
        vm(8, 512, dt=I32),
        pltpu.SMEM((8, 512), I32),
        many(NC + 1, *blkT),
        many(NR, *blkT),
        many(NR + 1, *blkT),
        many(NC, *blkT),
        many(32, *blkT),
        two(8), two(12), two(6), two(2), two(8), two(2),
        vm(512, 256), vm(512, 256),
        vm(8, 40, 256, dt=F32), vm(8, 40, 256, dt=F32), vm(4, 40, 256, dt=F32), vm(4, 40, 256, dt=F32),
        vm(8, 40, 256, dt=F32),
        pltpu.SemaphoreType.DMA((sems,)), pltpu.SemaphoreType.DMA((sems,)), pltpu.SemaphoreType.DMA((2 + H * BLK,)),
    ]
    vmem = pl.BlockSpec(memory_space=pltpu.VMEM)
    out, fg, dw, db = pl.pallas_call(
        functools.partial(kernel, H),
        out_shape=(
            jax.ShapeDtypeStruct((512, 256), BF16),
            jax.ShapeDtypeStruct((512, 256), BF16),
            jax.ShapeDtypeStruct((256, 256), F32),
            jax.ShapeDtypeStruct((1, 256), F32),
        ),
        in_specs=[pl.BlockSpec(memory_space=pl.ANY), vmem, vmem, pl.BlockSpec(memory_space=pl.ANY), vmem, vmem,
                  pl.BlockSpec(memory_space=pltpu.SMEM), vmem],
        out_specs=(vmem,) * 4,
        scratch_shapes=scratch,
        compiler_params=pltpu.CompilerParams(collective_id=0, has_side_effects=True, vmem_limit_bytes=60 << 20),
        name="layer",
    )(features, weight, bias.reshape(1, 256), tile_values, index, index.T, tile_count, out_grad)
    return out, fg, dw, db.reshape(256)


def solution(mesh):
    return jax.shard_map(
        functools.partial(shards, 1),
        mesh=mesh,
        in_specs=(
            P(("row", "col"), None),
            P(),
            P(),
            P("row", "col", None, None, None),
            P("row", "col", None, None),
            P("row", "col"),
            P(("row", "col"), None),
        ),
        out_specs=(P(("row", "col"), None), P(("row", "col"), None), P(), P()),
        check_vma=False,
    )
```

```python
import functools

import jax
import jax.numpy as jnp
from jax import lax
from jax.experimental import pallas as pl
from jax.experimental.pallas import tpu as pltpu
from jax.sharding import PartitionSpec as P

MESH = pl.DeviceIdType.MESH
TILE = 128
BLK = 4
SLOTS = 448
NR, NC = 32, 64
FPAIRS, BPAIRS = 240, 256
ZERO_RUN = 256
FUNROLL, BUNROLL = 24, 32
F32, BF16, I32 = jnp.float32, jnp.bfloat16, jnp.int32


def pair_lists(dst_r, dst_c, src_c, live_r, live_c, nd, ns):
    t_r = lax.broadcasted_iota(I32, (SLOTS, SLOTS), 1)
    t_c = lax.broadcasted_iota(I32, (SLOTS, SLOTS), 0)
    one = lambda m: m.astype(I32)
    dlive_r = jnp.where(live_r, dst_r, nd)
    dlive_c = jnp.where(live_c, dst_c, nd)
    own_cn = dlive_c == lax.broadcasted_iota(I32, (SLOTS, nd), 1)
    own_nr = dlive_r == lax.broadcasted_iota(I32, (nd, SLOTS), 0)
    n_r = jnp.sum(one(own_cn), axis=0, keepdims=True)
    n_c = jnp.sum(one(own_nr), axis=1, keepdims=True)
    half_c = (n_c + 1) // 2
    half_r = (n_r + 1) // 2
    g_c = lax.broadcasted_iota(I32, (nd, nd), 0)
    g_r = lax.broadcasted_iota(I32, (nd, nd), 1)
    base_r = jnp.sum(jnp.where(g_c < g_r, half_c, 0), axis=0, keepdims=True)
    base_c = jnp.sum(jnp.where(g_r < g_c, half_r, 0), axis=1, keepdims=True)
    rank_c = jnp.sum(one((dlive_c == dlive_r) & (t_r < t_c)), axis=1, keepdims=True)
    pos_c = jnp.sum(jnp.where(own_cn, 2 * base_r, 0), axis=1, keepdims=True) + rank_c
    pos_c = jnp.where(live_c, pos_c, 4096)
    hit = pos_c == lax.broadcasted_iota(I32, (SLOTS, 512), 1)
    slot = lax.broadcasted_iota(I32, (SLOTS, 512), 0)
    tile_l = jnp.sum(jnp.where(hit, slot, 0), axis=0, keepdims=True)
    src_l = jnp.sum(jnp.where(hit, src_c - ns, 0), axis=0, keepdims=True) + ns
    first = (base_c == lax.broadcasted_iota(I32, (nd, 512), 1)) & (n_c > 0)
    keep_l = 1 - jnp.sum(one(first), axis=0, keepdims=True)
    end_r = jnp.where(n_r > 0, base_r + half_r - 1, ZERO_RUN)
    return tile_l, src_l, keep_l, end_r


def kernel(H, feat, weight, bias, tiles_hbm, idx_r, cnt, ograd_hbm,
           output_hbm, fgrad_hbm, dw_hbm, db_hbm,
           ograd, output, fgrad, dw_out, db_out, tiles, runs, lists_v, lists, xs, ps, gs, qs, sib, rsa, rsb, rsa2, rsb2, sa, sb, ybf, zb,
           dbuf, drs, dp, dq, dfin, ss, rs, ls):
    w = 256 // H
    i, j = lax.axis_index("row"), lax.axis_index("col")
    y, xl, c = i // 4, lax.rem(i // 2, 2), lax.rem(i, 2)
    xh, z = j // 4, lax.rem(j, 4)
    m4 = lambda v: lax.rem(v + 4, 4)

    class Row:
        p, q = y, xl
        slot = staticmethod(lambda p, q: (p * 2 + q) * 2 + c)
        dev = staticmethod(lambda p, q: ((p * 2 + q) * 2 + c, j))

    class Col:
        p, q = z, xh
        slot = staticmethod(lambda p, q: q * 4 + p)
        dev = staticmethod(lambda p, q: (i, q * 4 + p))

    sibling = ((y * 2 + xl) * 2 + 1 - c, j)
    peers = [lax.rem(i + d, 16) for d in range(1, 16)]
    cpeers = [lax.rem(j + d, 8) for d in range(1, 8)]

    sent = []

    def send(src, dst, dev):
        n = len(sent)
        cp = pltpu.make_async_remote_copy(src_ref=src, dst_ref=dst, send_sem=ss.at[n], recv_sem=rs.at[n],
                                          device_id=dev, device_id_type=MESH)
        cp.start()
        sent.append(cp)
        return cp

    load_tiles = pltpu.make_async_copy(tiles_hbm.at[0, 0], tiles, ls.at[0])
    load_grad = pltpu.make_async_copy(ograd_hbm, ograd, ls.at[2 + H * BLK])
    loads = []
    for h in range(H):
        for t in range(BLK):
            cp = pltpu.make_async_copy(feat.at[pl.ds(t * TILE, TILE), pl.ds(h * w, w)], xs[h].at[i * BLK + t],
                                       ls.at[1 + h * BLK + t])
            cp.start()
            loads.append(cp)

    load_tiles.start()
    load_grad.start()
    barrier = pltpu.get_barrier_semaphore()
    for r in peers:
        pl.semaphore_signal(barrier, inc=1, device_id=(r, j), device_id_type=MESH)
    for k in cpeers:
        pl.semaphore_signal(barrier, inc=1, device_id=(i, k), device_id_type=MESH)
    pl.semaphore_wait(barrier, 22)
    for cp in loads:
        cp.wait()

    blk = lambda buf, s, lo=0, n=BLK: buf.at[pl.ds(s * BLK + lo, n)]

    def gather(g, buf, relay):
        p, q = g.p, g.q
        down = []

        def pass_on(s, lo, n):
            if relay:
                part = blk(buf, s, lo, n)
                down.append(send(part, part, sibling))

        def push(s, lo, n, dev):
            part = blk(buf, s, lo, n)
            return send(part, part, dev)

        me = g.slot(p, q)
        first = {d: push(me, 0, 2, g.dev(m4(p + d), q)) for d in (1, 3, 2)}
        cx = push(me, 0, BLK, g.dev(p, 1 - q))
        pass_on(me, 0, BLK)
        yield
        cx.wait_recv()
        other = g.slot(p, 1 - q)
        second = {d: push(me, 2, 2, g.dev(m4(p + d), q)) for d in (1, 3, 2)}
        third = {d: push(other, 2, 2, g.dev(m4(p + d), q)) for d in (1, 3, 2)}
        pass_on(other, 0, BLK)
        fourth = {}
        for d in (1, 3, 2):
            first[d].wait_recv()
            fourth[d] = push(g.slot(m4(p - d), q), 0, 2, g.dev(p, 1 - q))
        for d in (1, 3, 2):
            pass_on(g.slot(m4(p - d), q), 0, 2)
        yield
        for d in (1, 3, 2):
            second[d].wait_recv()
            pass_on(g.slot(m4(p - d), q), 2, 2)
        for d in (1, 3, 2):
            third[d].wait_recv()
            fourth[d].wait_recv()
            pass_on(g.slot(m4(p - d), 1 - q), 0, BLK)
        for cp in down:
            cp.wait_recv()

    def scatter(g, buf, k, h, emit):
        p, q = g.p, g.q
        ra, rb, ra2, rb2, oa, ob = rsa[k][h], rsb[k][h], rsa2[k][h], rsb2[k][h], sa[k][h], sb[k][h]
        xa, yb = {}, {}
        for d in (1, 3, 2, 0):
            xa[d] = send(blk(buf, g.slot(m4(p + d), 1 - q), 0, 2), ra.at[pl.ds(2 * d, 2)], g.dev(p, 1 - q))
        for d in (1, 3, 2):
            for e in (1, 0):
                qq = 1 - q if e else q
                yb[d, e] = send(blk(buf, g.slot(m4(p + d), qq), 2, 2), rb.at[pl.ds((d - 1) * 4 + e * 2, 2)],
                                g.dev(m4(p + d), q))
        yield
        y2 = {}
        for d in (1, 3, 2):
            xa[d].wait_recv()
            for t in range(2):
                own = buf[g.slot(m4(p + d), q) * BLK + t].astype(F32)
                oa[2 * d + t] = (own + ra[2 * d + t].astype(F32)).astype(BF16)
            y2[d] = send(oa.at[pl.ds(2 * d, 2)], ra2.at[pl.ds(2 * (d - 1), 2)], g.dev(m4(p + d), q))
        for d in (1, 3, 2):
            yb[d, 1].wait_recv()
        for t in range(2):
            tot = buf[g.slot(p, 1 - q) * BLK + 2 + t].astype(F32)
            for d in (1, 3, 2):
                tot = tot + rb[(d - 1) * 4 + 2 + t].astype(F32)
            ob[t] = tot.astype(BF16)
        x2 = send(ob, rb2, g.dev(p, 1 - q))
        yield
        xa[0].wait_recv()
        for d in (1, 3, 2):
            y2[d].wait_recv()
            yb[d, 0].wait_recv()
        for t in range(2):
            tot = buf[g.slot(p, q) * BLK + t].astype(F32) + ra[t].astype(F32)
            for d in (1, 3, 2):
                tot = tot + ra2[2 * (d - 1) + t].astype(F32)
            emit(t, tot)
        x2.wait_recv()
        for t in range(2):
            tot = buf[g.slot(p, q) * BLK + 2 + t].astype(F32)
            for d in (1, 3, 2):
                tot = tot + rb[(d - 1) * 4 + t].astype(F32)
            emit(2 + t, tot + rb2[t].astype(F32))

    def spmm(row, pairs, unroll, src, flip):
        axis = 0 if flip else 1

        def body(n, acc):
            for u in range(unroll):
                k = n * unroll + u
                left = jnp.concatenate([tiles[lists[row, 2 * k]], tiles[lists[row, 2 * k + 1]]], axis=axis)
                right = jnp.concatenate([src[lists[row + 1, 2 * k]], src[lists[row + 1, 2 * k + 1]]], axis=0)
                prod = lax.dot_general(left, right, (((axis,), (0,)), ((), ())), preferred_element_type=F32)
                acc = acc * lists[row + 2, k].astype(F32) + prod
                runs[k] = acc.astype(BF16)
            return acc

        lax.fori_loop(0, pairs // unroll, body, jnp.zeros((TILE, w), F32))

    def collect(row, nd, dst):
        def body(r, _):
            dst[r] = runs[lists[row + 3, r]]
            return 0

        lax.fori_loop(0, nd, body, 0)

    def finish(gen):
        for _ in gen:
            pass

    ag = [gather(Row, xs[h], True) for h in range(H)]
    next(ag[0])

    live_r = lax.broadcasted_iota(I32, (1, SLOTS), 1) < cnt[0, 0]
    live_c = lax.broadcasted_iota(I32, (SLOTS, 1), 0) < cnt[0, 0]
    idx_c = jnp.transpose(idx_r[...])
    r_r, c_r = idx_r[0:1, :], idx_r[1:2, :]
    r_c, c_c = idx_c[:, 0:1], idx_c[:, 1:2]
    lists_v[...] = jnp.zeros_like(lists_v)

    def put_lists(row, a, b, cc, nd, ns):
        t_l, s_l, k_l, e_l = pair_lists(a, b, cc, live_r, live_c, nd, ns)
        lists_v[row:row + 1, :] = t_l
        lists_v[row + 1:row + 2, :] = s_l
        lists_v[row + 2:row + 3, :] = k_l
        lists_v[row + 3:row + 4, 0:nd] = e_l

    put_lists(0, r_r, r_c, c_c, NR, NC)
    next(ag[0])
    for g in ag[1:]:
        next(g)
    put_lists(4, c_r, c_c, r_c, NC, NR)
    cp = pltpu.make_async_copy(lists_v, lists, ls.at[1 + H * BLK])
    cp.start()
    runs[ZERO_RUN] = jnp.zeros((TILE, w), BF16)
    for h in range(H):
        xs[h][NC] = jnp.zeros((TILE, w), BF16)
        gs[h][NR] = jnp.zeros((TILE, w), BF16)
    for g in ag[1:]:
        next(g)
    cp.wait()
    load_tiles.wait()

    def put_y(h):
        def emit(t, v):
            ybf[pl.ds(t * TILE, TILE), pl.ds(h * w, w)] = v.astype(BF16)
        return emit

    sc = []
    for h in range(H):
        finish(ag[h])
        spmm(0, FPAIRS, FUNROLL, xs[h], False)
        collect(0, NR, ps[h])
        g = scatter(Col, ps[h], 0, h, put_y(h))
        next(g)
        sc.append(g)
    for g in sc:
        next(g)
    for g in sc:
        finish(g)

    load_grad.wait()
    wb = weight[...]
    bsum = jnp.zeros((1, 256), F32)
    for t in range(BLK):
        rows = pl.ds(t * TILE, TILE)
        pre = jnp.dot(ybf[rows, :], wb, preferred_element_type=F32) + bias[...]
        sig = 1.0 / (1.0 + jnp.exp(-pre))
        output[rows, :] = (pre * sig).astype(BF16)
        slope = sig * (1.0 + pre * (1.0 - sig))
        pg = (ograd[rows, :].astype(F32) * slope).astype(BF16)
        bsum = bsum + jnp.sum(pg.astype(F32), axis=0, keepdims=True)
        zb[rows, :] = pg
        gw = lax.dot_general(pg, wb, (((1,), (1,)), ((), ())), preferred_element_type=F32).astype(BF16)
        for h in range(H):
            gs[h][j * BLK + t] = gw[:, h * w:(h + 1) * w]
    stores = [pltpu.make_async_copy(output, output_hbm, ls.at[3 + H * BLK])]
    stores[0].start()
    agc = [gather(Col, gs[h], False) for h in range(H)]
    next(agc[0])

    dw = lax.dot_general(ybf[...], zb[...], (((0,), (0,)), ((), ())), preferred_element_type=F32)
    for k in range(8):
        dbuf[k, 0:32, :] = dw[k * 32:(k + 1) * 32, :]
        dbuf[k, 32:40, :] = jnp.broadcast_to(bsum, (8, 256))
    drs[j] = dbuf[j]
    next(agc[0])
    for g in agc[1:]:
        next(g)
        next(g)
    s1 = [send(dbuf.at[lax.rem(j + d, 8)], drs.at[j], (i, lax.rem(j + d, 8))) for d in range(1, 8)]
    me4 = xl * 2 + c

    def grad_1():
        for cp in s1:
            cp.wait_recv()
        tot = drs[0]
        for k in range(1, 8):
            tot = tot + drs[k]
        dp[me4] = tot
        return [send(dp.at[me4], dp.at[me4], (y * 4 + lax.rem(me4 + d, 4), j)) for d in range(1, 4)]

    def grad_2(s2):
        for cp in s2:
            cp.wait_recv()
        dq[y] = (dp[0] + dp[1]) + (dp[2] + dp[3])
        return [send(dq.at[y], dq.at[y], (m4(y + d) * 4 + me4, j)) for d in (1, 3, 2)]

    def grad_3(s3):
        for cp in s3:
            cp.wait_recv()
        dfin[j] = (dq[0] + dq[1]) + (dq[2] + dq[3])
        return [send(dfin.at[j], dfin.at[j], (i, lax.rem(j + d, 8))) for d in range(1, 8)]

    def grad_4(s4):
        for cp in s4:
            cp.wait_recv()
        for k in range(8):
            dw_out[k * 32:(k + 1) * 32, :] = dfin[k, 0:32, :]
        db_out[...] = dfin[0, 32:33, :]
        for a, b, n in ((dw_out, dw_hbm, 4), (db_out, db_hbm, 5)):
            stores.append(pltpu.make_async_copy(a, b, ls.at[n + H * BLK]))
            stores[-1].start()

    def put_f(h):
        def emit(t, v):
            fgrad[pl.ds(t * TILE, TILE), pl.ds(h * w, w)] = v.astype(BF16)
        return emit

    def to_sibling(h):
        cps = []
        for k in range(8):
            cps.append(send(blk(qs[h], k * 2 + 1 - c), sib[h].at[pl.ds(k * BLK, BLK)], sibling))
        return cps

    def combine(h, cps):
        for k in range(8):
            cps[k].wait_recv()
            for t in range(BLK):
                at = (k * 2 + c) * BLK + t
                qs[h][at] = (qs[h][at].astype(F32) + sib[h][k * BLK + t].astype(F32)).astype(BF16)

    back = []
    finish(agc[0])
    for h in range(H):
        spmm(4, BPAIRS, BUNROLL, gs[h], True)
        collect(4, NC, qs[h])
        cps = to_sibling(h)
        if h == 0:
            s2 = grad_1()
        else:
            next(back[0])
        if h == H - 1:
            s3 = grad_2(s2)
        else:
            finish(agc[1])
        combine(h, cps)
        g = scatter(Row, qs[h], 1, h, put_f(h))
        next(g)
        back.append(g)
    s4 = grad_3(s3)
    next(back[-1])
    for g in back:
        finish(g)
    stores.append(pltpu.make_async_copy(fgrad, fgrad_hbm, ls.at[6 + H * BLK]))
    stores[-1].start()
    grad_4(s4)
    for cp in stores:
        cp.wait()
    for cp in sent:
        cp.wait_send()


def tail(*refs):
    src, dst, mid, sem = refs[:4], refs[4:8], refs[8:12], refs[12]
    first = [pltpu.make_async_copy(src[n], mid[n], sem.at[n]) for n in range(4)]
    second = [pltpu.make_async_copy(mid[n], dst[n], sem.at[4 + n]) for n in range(4)]
    for cp in first:
        cp.start()
    for n in range(4):
        first[n].wait()
        second[n].start()
    for cp in second:
        cp.wait()


def shards(H, features, weight, bias, tile_values, tile_index, tile_count, out_grad):
    w = 256 // H
    vm = lambda *s, dt=BF16: pltpu.VMEM(s, dt)
    many = lambda n, *s: [vm(n, *s)] * H
    blkT = (TILE, w)
    two = lambda n: [many(n, *blkT) for _ in range(2)]
    index_t = tile_index[0, 0].T
    sems = 180
    scratch = [
        vm(512, 256), vm(512, 256), vm(512, 256),
        vm(256, 256, dt=F32), vm(1, 256, dt=F32),
        vm(SLOTS, TILE, TILE),
        vm(ZERO_RUN + 1, *blkT),
        vm(8, 512, dt=I32),
        pltpu.SMEM((8, 512), I32),
        many(NC + 1, *blkT),
        many(NR, *blkT),
        many(NR + 1, *blkT),
        many(NC, *blkT),
        many(32, *blkT),
        two(8), two(12), two(6), two(2), two(8), two(2),
        vm(512, 256), vm(512, 256),
        vm(8, 40, 256, dt=F32), vm(8, 40, 256, dt=F32), vm(4, 40, 256, dt=F32), vm(4, 40, 256, dt=F32),
        vm(8, 40, 256, dt=F32),
        pltpu.SemaphoreType.DMA((sems,)), pltpu.SemaphoreType.DMA((sems,)), pltpu.SemaphoreType.DMA((7 + H * BLK,)),
    ]
    vmem = pl.BlockSpec(memory_space=pltpu.VMEM)
    hbm = pl.BlockSpec(memory_space=pl.ANY)
    shapes = (
        jax.ShapeDtypeStruct((512, 256), BF16),
        jax.ShapeDtypeStruct((512, 256), BF16),
        jax.ShapeDtypeStruct((256, 256), F32),
        jax.ShapeDtypeStruct((1, 256), F32),
    )
    results = pl.pallas_call(
        functools.partial(kernel, H),
        out_shape=shapes,
        in_specs=[hbm, vmem, vmem, hbm, vmem, pl.BlockSpec(memory_space=pltpu.SMEM), hbm],
        out_specs=(hbm,) * 4,
        scratch_shapes=scratch,
        compiler_params=pltpu.CompilerParams(collective_id=0, has_side_effects=True, vmem_limit_bytes=60 << 20),
        name="layer",
    )(features, weight, bias.reshape(1, 256), tile_values, index_t, tile_count, out_grad)
    out, fg, dw, db = pl.pallas_call(
        tail,
        out_shape=shapes,
        in_specs=[hbm] * 4,
        out_specs=(hbm,) * 4,
        scratch_shapes=[pltpu.VMEM(x.shape, x.dtype) for x in shapes] + [pltpu.SemaphoreType.DMA((8,))],
        compiler_params=pltpu.CompilerParams(vmem_limit_bytes=60 << 20),
        name="results",
    )(*results)
    return out, fg, dw, db.reshape(256)


def solution(mesh):
    return jax.shard_map(
        functools.partial(shards, 2),
        mesh=mesh,
        in_specs=(
            P(("row", "col"), None),
            P(),
            P(),
            P("row", "col", None, None, None),
            P("row", "col", None, None),
            P("row", "col"),
            P(("row", "col"), None),
        ),
        out_specs=(P(("row", "col"), None), P(("row", "col"), None), P(), P()),
        check_vma=False,
    )
```

```python
import functools

import jax
import jax.numpy as jnp
from jax import lax
from jax.experimental import pallas as pl
from jax.experimental.pallas import tpu as pltpu
from jax.sharding import PartitionSpec as P

MESH = pl.DeviceIdType.MESH
TILE = 128
BLK = 4
SLOTS = 448
NR, NC = 32, 64
FPAIRS, BPAIRS = 240, 256
ZERO_RUN = 256
FUNROLL, BUNROLL = 48, 64
F32, BF16, I32 = jnp.float32, jnp.bfloat16, jnp.int32


def pair_lists(dst_r, dst_c, src_c, live_r, live_c, nd, ns):
    t_r = lax.broadcasted_iota(I32, (SLOTS, SLOTS), 1)
    t_c = lax.broadcasted_iota(I32, (SLOTS, SLOTS), 0)
    one = lambda m: m.astype(I32)
    dlive_r = jnp.where(live_r, dst_r, nd)
    dlive_c = jnp.where(live_c, dst_c, nd)
    own_cn = dlive_c == lax.broadcasted_iota(I32, (SLOTS, nd), 1)
    own_nr = dlive_r == lax.broadcasted_iota(I32, (nd, SLOTS), 0)
    n_r = jnp.sum(one(own_cn), axis=0, keepdims=True)
    n_c = jnp.sum(one(own_nr), axis=1, keepdims=True)
    half_c = (n_c + 1) // 2
    half_r = (n_r + 1) // 2
    g_c = lax.broadcasted_iota(I32, (nd, nd), 0)
    g_r = lax.broadcasted_iota(I32, (nd, nd), 1)
    base_r = jnp.sum(jnp.where(g_c < g_r, half_c, 0), axis=0, keepdims=True)
    base_c = jnp.sum(jnp.where(g_r < g_c, half_r, 0), axis=1, keepdims=True)
    rank_c = jnp.sum(one((dlive_c == dlive_r) & (t_r < t_c)), axis=1, keepdims=True)
    pos_c = jnp.sum(jnp.where(own_cn, 2 * base_r, 0), axis=1, keepdims=True) + rank_c
    pos_c = jnp.where(live_c, pos_c, 4096)
    hit = pos_c == lax.broadcasted_iota(I32, (SLOTS, 512), 1)
    slot = lax.broadcasted_iota(I32, (SLOTS, 512), 0)
    tile_l = jnp.sum(jnp.where(hit, slot, 0), axis=0, keepdims=True)
    src_l = jnp.sum(jnp.where(hit, src_c - ns, 0), axis=0, keepdims=True) + ns
    first = (base_c == lax.broadcasted_iota(I32, (nd, 512), 1)) & (n_c > 0)
    keep_l = 1 - jnp.sum(one(first), axis=0, keepdims=True)
    end_r = jnp.where(n_r > 0, base_r + half_r - 1, ZERO_RUN)
    return tile_l, src_l, keep_l, end_r


def kernel(H, feat, weight_hbm, bias_hbm, tiles_hbm, idx_hbm, cnt, ograd_hbm,
           output_hbm, fgrad_hbm, dw_hbm, db_hbm,
           weight, bias, idx_r, ograd, output, fgrad, dw_out, db_out, tiles, runs, lists_v, lists, xs, ps, gs, qs, sib, rsa, rsb, rsa2, rsb2, sa, sb, ybf, zb,
           dbuf, dsib, dsum, drs, dp, dfin, ss, rs, ls):
    w = 256 // H
    i, j = lax.axis_index("row"), lax.axis_index("col")
    y, xl, c = i // 4, lax.rem(i // 2, 2), lax.rem(i, 2)
    xh, z = j // 4, lax.rem(j, 4)
    m4 = lambda v: lax.rem(v + 4, 4)

    class Row:
        p, q = y, xl
        slot = staticmethod(lambda p, q: (p * 2 + q) * 2 + c)
        dev = staticmethod(lambda p, q: ((p * 2 + q) * 2 + c, j))

    class Col:
        p, q = z, xh
        slot = staticmethod(lambda p, q: q * 4 + p)
        dev = staticmethod(lambda p, q: (i, q * 4 + p))

    sibling = ((y * 2 + xl) * 2 + 1 - c, j)
    peers = [lax.rem(i + d, 16) for d in range(1, 16)]
    cpeers = [lax.rem(j + d, 8) for d in range(1, 8)]

    sent = []

    def send(src, dst, dev):
        n = len(sent)
        cp = pltpu.make_async_remote_copy(src_ref=src, dst_ref=dst, send_sem=ss.at[n], recv_sem=rs.at[n],
                                          device_id=dev, device_id_type=MESH)
        cp.start()
        sent.append(cp)
        return cp

    load_tiles = pltpu.make_async_copy(tiles_hbm.at[0, 0], tiles, ls.at[0])
    load_grad = pltpu.make_async_copy(ograd_hbm, ograd, ls.at[2 + H * BLK])
    loads = []
    for h in range(H):
        for t in range(BLK):
            cp = pltpu.make_async_copy(feat.at[pl.ds(t * TILE, TILE), pl.ds(h * w, w)], xs[h].at[i * BLK + t],
                                       ls.at[1 + h * BLK + t])
            cp.start()
            loads.append(cp)

    small = []
    for n, (a, b) in enumerate(((idx_hbm, idx_r), (weight_hbm, weight), (bias_hbm, bias))):
        small.append(pltpu.make_async_copy(a, b, ls.at[7 + H * BLK + n]))
        small[-1].start()
    load_grad.start()
    load_tiles.start()
    barrier = pltpu.get_barrier_semaphore()
    for r in peers:
        pl.semaphore_signal(barrier, inc=1, device_id=(r, j), device_id_type=MESH)
    for k in cpeers:
        pl.semaphore_signal(barrier, inc=1, device_id=(i, k), device_id_type=MESH)
    pl.semaphore_wait(barrier, 22)
    for cp in loads:
        cp.wait()

    blk = lambda buf, s, lo=0, n=BLK: buf.at[pl.ds(s * BLK + lo, n)]

    def gather(g, buf, relay):
        p, q = g.p, g.q
        down = []

        def pass_on(s, lo, n):
            if relay:
                part = blk(buf, s, lo, n)
                down.append(send(part, part, sibling))

        def push(s, lo, n, dev):
            part = blk(buf, s, lo, n)
            return send(part, part, dev)

        me, other = g.slot(p, q), g.slot(p, 1 - q)
        e = 1 - 2 * c
        sides = (1, 3)
        near = {d: g.slot(m4(p - d), q) for d in sides}
        cross = g.dev(p, 1 - q)
        ahead = g.dev(m4(p + e), q)
        around = lambda s, lo: [push(s, lo, 2, g.dev(m4(p + d), q)) for d in sides]

        def arrived(copies):
            for cp in copies:
                cp.wait_recv()

        cx = push(me, 2, 2, cross)
        f1 = around(me, 0)
        cx2 = push(me, 0, 2, cross)
        pass_on(me, 0, BLK)
        f2 = around(me, 2)
        yield
        cx.wait_recv()
        f3 = around(other, 2)
        arrived(f1)
        w1 = push(g.slot(m4(p - e), q), 0, 2, ahead)
        x1 = [push(near[d], 0, 2, cross) for d in sides]
        yield
        arrived(f2)
        w2 = push(g.slot(m4(p - e), q), 2, 2, ahead)
        for d in sides:
            pass_on(near[d], 0, BLK)
        cx2.wait_recv()
        pass_on(other, 0, BLK)
        w1.wait_recv()
        x2 = push(g.slot(m4(p + 2), q), 0, 2, cross)
        arrived(f3)
        w3 = push(g.slot(m4(p - e), 1 - q), 2, 2, ahead)
        yield
        w2.wait_recv()
        pass_on(g.slot(m4(p + 2), q), 0, BLK)
        for u, d in zip(x1, sides):
            u.wait_recv()
            pass_on(g.slot(m4(p - d), 1 - q), 0, BLK)
        w3.wait_recv()
        x2.wait_recv()
        pass_on(g.slot(m4(p + 2), 1 - q), 0, BLK)
        yield
        for cp in down:
            cp.wait_recv()

    def scatter(g, buf, k, h, emit, ready):
        p, q = g.p, g.q
        ra, rb, ra2, rb2, oa, ob = rsa[k][h], rsb[k][h], rsa2[k][h], rsb2[k][h], sa[k][h], sb[k][h]
        xa, yb = {}, {}
        for d in (1, 3, 2, 0):
            for f in (1, 0):
                s = g.slot(m4(p + d), 1 - q if f else q)
                ready(d, f, s)
                if f:
                    xa[d] = send(blk(buf, s, 0, 2), ra.at[pl.ds(2 * d, 2)], g.dev(p, 1 - q))
                if d:
                    yb[d, f] = send(blk(buf, s, 2, 2), rb.at[pl.ds((d - 1) * 4 + f * 2, 2)], g.dev(m4(p + d), q))
        yield
        y2 = {}
        for d in (1, 3, 2):
            xa[d].wait_recv()
            for t in range(2):
                own = buf[g.slot(m4(p + d), q) * BLK + t].astype(F32)
                oa[2 * d + t] = (own + ra[2 * d + t].astype(F32)).astype(BF16)
            y2[d] = send(oa.at[pl.ds(2 * d, 2)], ra2.at[pl.ds(2 * (d - 1), 2)], g.dev(m4(p + d), q))
        for d in (1, 3, 2):
            yb[d, 1].wait_recv()
        for t in range(2):
            tot = buf[g.slot(p, 1 - q) * BLK + 2 + t].astype(F32)
            for d in (1, 3, 2):
                tot = tot + rb[(d - 1) * 4 + 2 + t].astype(F32)
            ob[t] = tot.astype(BF16)
        x2 = send(ob, rb2, g.dev(p, 1 - q))
        yield
        xa[0].wait_recv()
        for d in (1, 3, 2):
            y2[d].wait_recv()
            yb[d, 0].wait_recv()
        for t in range(2):
            tot = buf[g.slot(p, q) * BLK + t].astype(F32) + ra[t].astype(F32)
            for d in (1, 3, 2):
                tot = tot + ra2[2 * (d - 1) + t].astype(F32)
            emit(t, tot)
        x2.wait_recv()
        for t in range(2):
            tot = buf[g.slot(p, q) * BLK + 2 + t].astype(F32)
            for d in (1, 3, 2):
                tot = tot + rb[(d - 1) * 4 + t].astype(F32)
            emit(2 + t, tot + rb2[t].astype(F32))

    def spmm(row, lo, hi, unroll, src, flip, acc=None):
        axis = 0 if flip else 1

        def body(n, acc):
            for u in range(unroll):
                k = n * unroll + u
                left = jnp.concatenate([tiles[lists[row, 2 * k]], tiles[lists[row, 2 * k + 1]]], axis=axis)
                right = jnp.concatenate([src[lists[row + 1, 2 * k]], src[lists[row + 1, 2 * k + 1]]], axis=0)
                prod = lax.dot_general(left, right, (((axis,), (0,)), ((), ())), preferred_element_type=F32)
                acc = acc * lists[row + 2, k].astype(F32) + prod
                runs[k] = acc.astype(BF16)
            return acc

        return lax.fori_loop(lo, hi, body, jnp.zeros((TILE, w), F32) if acc is None else acc)

    def collect(row, slot, dst):
        def body(t, _):
            dst[slot * BLK + t] = runs[lists[row + 3, slot * BLK + t]]
            return 0

        lax.fori_loop(0, BLK, body, 0)

    def finish(gen):
        for _ in gen:
            pass

    ag = [gather(Row, xs[h], True) for h in range(H)]
    next(ag[0])

    for cp in small:
        cp.wait()
    live_r = lax.broadcasted_iota(I32, (1, SLOTS), 1) < cnt[...]
    live_c = lax.broadcasted_iota(I32, (SLOTS, 1), 0) < cnt[...]
    idx_c = jnp.transpose(idx_r[...])
    r_r, c_r = idx_r[0:1, :], idx_r[1:2, :]
    r_c, c_c = idx_c[:, 0:1], idx_c[:, 1:2]
    lists_v[...] = jnp.zeros_like(lists_v)

    def put_lists(row, a, b, cc, nd, ns):
        t_l, s_l, k_l, e_l = pair_lists(a, b, cc, live_r, live_c, nd, ns)
        lists_v[row:row + 1, :] = t_l
        lists_v[row + 1:row + 2, :] = s_l
        lists_v[row + 2:row + 3, :] = k_l
        lists_v[row + 3:row + 4, 0:nd] = e_l

    put_lists(0, r_r, r_c, c_c, NR, NC)
    next(ag[0])
    for g in ag[1:]:
        next(g)
    next(ag[0])
    for g in ag[1:]:
        next(g)
    put_lists(4, c_r, c_c, r_c, NC, NR)
    cp = pltpu.make_async_copy(lists_v, lists, ls.at[1 + H * BLK])
    cp.start()
    runs[ZERO_RUN] = jnp.zeros((TILE, w), BF16)
    for h in range(H):
        xs[h][NC] = jnp.zeros((TILE, w), BF16)
        gs[h][NR] = jnp.zeros((TILE, w), BF16)
    next(ag[0])
    for g in ag[1:]:
        next(g)
    cp.wait()
    load_tiles.wait()

    def put_y(h):
        def emit(t, v):
            ybf[pl.ds(t * TILE, TILE), pl.ds(h * w, w)] = v.astype(BF16)
        return emit

    sc = []
    for h in range(H):
        finish(ag[h])
        turns = FPAIRS // FUNROLL
        acc = spmm(0, 0, turns - 1, FUNROLL, xs[h], False)
        if h + 1 < H:
            next(ag[h + 1])
        spmm(0, turns - 1, turns, FUNROLL, xs[h], False, acc)
        g = scatter(Col, ps[h], 0, h, put_y(h), lambda d, f, s: collect(0, s, ps[h]))
        next(g)
        sc.append(g)
    for g in sc:
        next(g)
    for g in sc:
        finish(g)

    load_grad.wait()
    wb = weight[...]
    bsum = jnp.zeros((1, 256), F32)
    for t in range(BLK):
        rows = pl.ds(t * TILE, TILE)
        pre = jnp.dot(ybf[rows, :], wb, preferred_element_type=F32) + bias[...]
        sig = 1.0 / (1.0 + jnp.exp(-pre))
        output[rows, :] = (pre * sig).astype(BF16)
        slope = sig * (1.0 + pre * (1.0 - sig))
        pg = (ograd[rows, :].astype(F32) * slope).astype(BF16)
        bsum = bsum + jnp.sum(pg.astype(F32), axis=0, keepdims=True)
        zb[rows, :] = pg
        gw = lax.dot_general(pg, wb, (((1,), (1,)), ((), ())), preferred_element_type=F32).astype(BF16)
        for h in range(H):
            gs[h][j * BLK + t] = gw[:, h * w:(h + 1) * w]
    stores = [pltpu.make_async_copy(output, output_hbm, ls.at[3 + H * BLK])]
    stores[0].start()
    agc = [gather(Col, gs[h], False) for h in range(H)]
    next(agc[0])

    dw = lax.dot_general(ybf[...], zb[...], (((0,), (0,)), ((), ())), preferred_element_type=F32)
    for k in range(16):
        dbuf[k, 0:16, :] = dw[k * 16:(k + 1) * 16, :]
        dbuf[k, 16:24, :] = jnp.broadcast_to(bsum, (8, 256))
    s0 = send(dbuf.at[pl.ds((1 - c) * 8, 8)], dsib, sibling)
    next(agc[0])
    for g in agc[1:]:
        next(g)
    next(agc[0])
    for g in agc[1:]:
        next(g)
    next(agc[0])
    for g in agc[1:]:
        next(g)
    s0.wait_recv()
    for k in range(8):
        dsum[k] = dbuf[c * 8 + k] + dsib[k]
    drs[j] = dsum[j]
    chip = y * 2 + xl

    def total(ref):
        tot = ref[0]
        for k in range(1, 8):
            tot = tot + ref[k]
        return tot

    def grad_0():
        return [send(dsum.at[lax.rem(j + d, 8)], drs.at[j], (i, lax.rem(j + d, 8))) for d in range(1, 8)]

    def grad_1(s1):
        for cp in s1:
            cp.wait_recv()
        dp[chip] = total(drs)
        return [send(dp.at[chip], dp.at[chip], (lax.rem(chip + d, 8) * 2 + c, j)) for d in range(1, 8)]

    def grad_2(s2):
        for cp in s2:
            cp.wait_recv()
        dfin[c * 8 + j] = total(dp)
        return [send(dfin.at[c * 8 + j], dfin.at[c * 8 + j], (i, lax.rem(j + d, 8))) for d in range(1, 8)]

    def grad_3(s3):
        for cp in s3:
            cp.wait_recv()
        half = dfin.at[pl.ds(c * 8, 8)]
        return send(half, half, sibling)

    def grad_4(s4):
        s4.wait_recv()
        for k in range(16):
            dw_out[k * 16:(k + 1) * 16, :] = dfin[k, 0:16, :]
        db_out[...] = dfin[0, 16:17, :]
        for a, b, n in ((dw_out, dw_hbm, 4), (db_out, db_hbm, 5)):
            stores.append(pltpu.make_async_copy(a, b, ls.at[n + H * BLK]))
            stores[-1].start()

    def put_f(h):
        def emit(t, v):
            fgrad[pl.ds(t * TILE, TILE), pl.ds(h * w, w)] = v.astype(BF16)
        return emit

    def to_sibling(h):
        cps = {}
        chips = [(d, f, m4(y + d) * 2 + (1 - xl if f else xl)) for d in (1, 3, 2, 0) for f in (1, 0)]
        for d, f, k in chips:
            collect(4, k * 2 + 1 - c, qs[h])
            cps[d, f] = send(blk(qs[h], k * 2 + 1 - c), sib[h].at[pl.ds(k * BLK, BLK)], sibling)
        for d, f, k in chips:
            collect(4, k * 2 + c, qs[h])
        return cps

    def combine(h, cp, s):
        cp.wait_recv()

        def body(t, _):
            at = s * BLK + t
            qs[h][at] = (qs[h][at].astype(F32) + sib[h][(s - c) * 2 + t].astype(F32)).astype(BF16)
            return 0

        lax.fori_loop(0, BLK, body, 0)

    back = []
    finish(agc[0])
    def row_stage(h, cps):
        g = scatter(Row, qs[h], 1, h, put_f(h), lambda d, f, s: combine(h, cps[d, f], s))
        next(g)
        back.append(g)

    turns = BPAIRS // BUNROLL
    for h in range(H):
        acc = spmm(4, 0, turns // 2, BUNROLL, gs[h], True)
        if h > 0:
            row_stage(0, cps)
            s2 = grad_1(s1)
        elif H == 1:
            s1 = grad_0()
        spmm(4, turns // 2, turns, BUNROLL, gs[h], True, acc)
        cps = to_sibling(h)
        if h + 1 < H:
            finish(agc[h + 1])
            s1 = grad_0()
    if H == 1:
        s2 = grad_1(s1)
    row_stage(H - 1, cps)
    s3 = grad_2(s2)
    for g in back:
        next(g)
    s4 = grad_3(s3)
    for g in back:
        finish(g)
    stores.append(pltpu.make_async_copy(fgrad, fgrad_hbm, ls.at[6 + H * BLK]))
    stores[-1].start()
    grad_4(s4)
    for cp in stores:
        cp.wait()
    for cp in sent:
        cp.wait_send()


def tail(*refs):
    src, dst, mid, sem = refs[:4], refs[4:8], refs[8:12], refs[12]
    first = [pltpu.make_async_copy(src[n], mid[n], sem.at[n]) for n in range(4)]
    second = [pltpu.make_async_copy(mid[n], dst[n], sem.at[4 + n]) for n in range(4)]
    for cp in first:
        cp.start()
    for n in range(4):
        first[n].wait()
        second[n].start()
    for cp in second:
        cp.wait()


def shards(H, features, weight, bias, tile_values, tile_index, tile_count, out_grad):
    w = 256 // H
    vm = lambda *s, dt=BF16: pltpu.VMEM(s, dt)
    many = lambda n, *s: [vm(n, *s)] * H
    blkT = (TILE, w)
    two = lambda n: [many(n, *blkT) for _ in range(2)]
    index_t = tile_index[0, 0].T
    sems = 180
    scratch = [
        vm(256, 256), vm(1, 256, dt=F32), vm(2, SLOTS, dt=I32),
        vm(512, 256), vm(512, 256), vm(512, 256),
        vm(256, 256, dt=F32), vm(1, 256, dt=F32),
        vm(SLOTS, TILE, TILE),
        vm(ZERO_RUN + 1, *blkT),
        vm(8, 512, dt=I32),
        pltpu.SMEM((8, 512), I32),
        many(NC + 1, *blkT),
        many(NR, *blkT),
        many(NR + 1, *blkT),
        many(NC, *blkT),
        many(32, *blkT),
        two(8), two(12), two(6), two(2), two(8), two(2),
        vm(512, 256), vm(512, 256),
        vm(16, 24, 256, dt=F32), vm(8, 24, 256, dt=F32), vm(8, 24, 256, dt=F32), vm(8, 24, 256, dt=F32),
        vm(8, 24, 256, dt=F32), vm(16, 24, 256, dt=F32),
        pltpu.SemaphoreType.DMA((sems,)), pltpu.SemaphoreType.DMA((sems,)), pltpu.SemaphoreType.DMA((11 + H * BLK,)),
    ]
    hbm = pl.BlockSpec(memory_space=pl.ANY)
    shapes = (
        jax.ShapeDtypeStruct((512, 256), BF16),
        jax.ShapeDtypeStruct((512, 256), BF16),
        jax.ShapeDtypeStruct((256, 256), F32),
        jax.ShapeDtypeStruct((1, 256), F32),
    )
    results = pl.pallas_call(
        functools.partial(kernel, H),
        out_shape=shapes,
        in_specs=[hbm] * 5 + [pl.BlockSpec(memory_space=pltpu.VMEM), hbm],
        out_specs=(hbm,) * 4,
        scratch_shapes=scratch,
        compiler_params=pltpu.CompilerParams(collective_id=0, has_side_effects=True, vmem_limit_bytes=60 << 20),
        name="layer",
    )(features, weight, bias.reshape(1, 256), tile_values, index_t, tile_count, out_grad)
    out, fg, dw, db = pl.pallas_call(
        tail,
        out_shape=shapes,
        in_specs=[hbm] * 4,
        out_specs=(hbm,) * 4,
        scratch_shapes=[pltpu.VMEM(x.shape, x.dtype) for x in shapes] + [pltpu.SemaphoreType.DMA((8,))],
        compiler_params=pltpu.CompilerParams(vmem_limit_bytes=60 << 20),
        name="results",
    )(*results)
    return out, fg, dw, db.reshape(256)


def solution(mesh):
    return jax.shard_map(
        functools.partial(shards, 2),
        mesh=mesh,
        in_specs=(
            P(("row", "col"), None),
            P(),
            P(),
            P("row", "col", None, None, None),
            P("row", "col", None, None),
            P("row", "col"),
            P(("row", "col"), None),
        ),
        out_specs=(P(("row", "col"), None), P(("row", "col"), None), P(), P()),
        check_vma=False,
    )
```

```python
import functools

import jax
import jax.numpy as jnp
from jax import lax
from jax.experimental import pallas as pl
from jax.experimental.pallas import tpu as pltpu
from jax.sharding import PartitionSpec as P

MESH = pl.DeviceIdType.MESH
TILE = 128
BLK = 4
SLOTS = 448
NR, NC = 32, 64
FPAIRS, BPAIRS = 240, 256
ZERO_RUN = 256
FUNROLL, BUNROLL = 80, 128
F32, BF16, I32 = jnp.float32, jnp.bfloat16, jnp.int32


def pair_lists(dst_r, dst_c, src_c, live_r, live_c, nd, ns):
    t_r = lax.broadcasted_iota(I32, (SLOTS, SLOTS), 1)
    t_c = lax.broadcasted_iota(I32, (SLOTS, SLOTS), 0)
    one = lambda m: m.astype(I32)
    dlive_r = jnp.where(live_r, dst_r, nd)
    dlive_c = jnp.where(live_c, dst_c, nd)
    own_cn = dlive_c == lax.broadcasted_iota(I32, (SLOTS, nd), 1)
    own_nr = dlive_r == lax.broadcasted_iota(I32, (nd, SLOTS), 0)
    n_r = jnp.sum(one(own_cn), axis=0, keepdims=True)
    n_c = jnp.sum(one(own_nr), axis=1, keepdims=True)
    half_c = (n_c + 1) // 2
    half_r = (n_r + 1) // 2
    g_c = lax.broadcasted_iota(I32, (nd, nd), 0)
    g_r = lax.broadcasted_iota(I32, (nd, nd), 1)
    base_r = jnp.sum(jnp.where(g_c < g_r, half_c, 0), axis=0, keepdims=True)
    base_c = jnp.sum(jnp.where(g_r < g_c, half_r, 0), axis=1, keepdims=True)
    rank_c = jnp.sum(one((dlive_c == dlive_r) & (t_r < t_c)), axis=1, keepdims=True)
    pos_c = jnp.sum(jnp.where(own_cn, 2 * base_r, 0), axis=1, keepdims=True) + rank_c
    pos_c = jnp.where(live_c, pos_c, 4096)
    hit = pos_c == lax.broadcasted_iota(I32, (SLOTS, 512), 1)
    slot = lax.broadcasted_iota(I32, (SLOTS, 512), 0)
    tile_l = jnp.sum(jnp.where(hit, slot, 0), axis=0, keepdims=True)
    src_l = jnp.sum(jnp.where(hit, src_c - ns, 0), axis=0, keepdims=True) + ns
    first = (base_c == lax.broadcasted_iota(I32, (nd, 512), 1)) & (n_c > 0)
    keep_l = 1 - jnp.sum(one(first), axis=0, keepdims=True)
    end_r = jnp.where(n_r > 0, base_r + half_r - 1, ZERO_RUN)
    return tile_l, src_l, keep_l, end_r


def kernel(H, feat, weight_hbm, bias_hbm, tiles_hbm, idx_hbm, cnt, ograd_hbm,
           output_hbm, fgrad_hbm, dw_hbm, db_hbm,
           weight, bias, idx_r, ograd, output, fgrad, dw_out, db_out, tiles, runs, lists_v, lists, xs, ps, gs, qs, sib, rsa, rsb, rsa2, rsb2, sa, sb, ybf, zb,
           dbuf, dsib, dsum, drs, dp, dfin, ss, rs, ls):
    w = 256 // H
    i, j = lax.axis_index("row"), lax.axis_index("col")
    y, xl, c = i // 4, lax.rem(i // 2, 2), lax.rem(i, 2)
    xh, z = j // 4, lax.rem(j, 4)
    m4 = lambda v: lax.rem(v + 4, 4)

    class Row:
        p, q = y, xl
        slot = staticmethod(lambda p, q: (p * 2 + q) * 2 + c)
        dev = staticmethod(lambda p, q: ((p * 2 + q) * 2 + c, j))

    class Col:
        p, q = z, xh
        slot = staticmethod(lambda p, q: q * 4 + p)
        dev = staticmethod(lambda p, q: (i, q * 4 + p))

    sibling = ((y * 2 + xl) * 2 + 1 - c, j)
    peers = [lax.rem(i + d, 16) for d in range(1, 16)]
    cpeers = [lax.rem(j + d, 8) for d in range(1, 8)]

    sent, drained = [], [0]

    def send(src, dst, dev):
        n = len(sent)
        cp = pltpu.make_async_remote_copy(src_ref=src, dst_ref=dst, send_sem=ss.at[n], recv_sem=rs.at[n],
                                          device_id=dev, device_id_type=MESH)
        cp.start()
        sent.append(cp)
        return cp

    def drain(until):
        for cp in sent[drained[0]:until]:
            cp.wait_send()
        drained[0] = until

    load_tiles = pltpu.make_async_copy(tiles_hbm.at[0, 0], tiles, ls.at[0])
    load_grad = pltpu.make_async_copy(ograd_hbm, ograd, ls.at[2 + H * BLK])
    loads = []
    for h in range(H):
        for t in range(BLK):
            cp = pltpu.make_async_copy(feat.at[pl.ds(t * TILE, TILE), pl.ds(h * w, w)], xs[h].at[i * BLK + t],
                                       ls.at[1 + h * BLK + t])
            cp.start()
            loads.append(cp)

    small = []
    for n, (a, b) in enumerate(((idx_hbm, idx_r), (weight_hbm, weight), (bias_hbm, bias))):
        small.append(pltpu.make_async_copy(a, b, ls.at[8 + H * BLK + n]))
        small[-1].start()
    load_grad.start()
    load_tiles.start()
    barrier = pltpu.get_barrier_semaphore()
    for r in peers:
        pl.semaphore_signal(barrier, inc=1, device_id=(r, j), device_id_type=MESH)
    for k in cpeers:
        pl.semaphore_signal(barrier, inc=1, device_id=(i, k), device_id_type=MESH)
    pl.semaphore_wait(barrier, 22)
    for cp in loads:
        cp.wait()

    blk = lambda buf, s, lo=0, n=BLK: buf.at[pl.ds(s * BLK + lo, n)]

    def gather(g, buf, relay):
        p, q = g.p, g.q
        down = []

        def pass_on(s, lo, n):
            if relay:
                part = blk(buf, s, lo, n)
                down.append(send(part, part, sibling))

        def push(s, lo, n, dev):
            part = blk(buf, s, lo, n)
            return send(part, part, dev)

        me, other = g.slot(p, q), g.slot(p, 1 - q)
        e = 1 - 2 * c
        sides = (1, 3)
        near = {d: g.slot(m4(p - d), q) for d in sides}
        cross = g.dev(p, 1 - q)
        ahead = g.dev(m4(p + e), q)
        around = lambda s, lo: [push(s, lo, 2, g.dev(m4(p + d), q)) for d in sides]

        def arrived(copies):
            for cp in copies:
                cp.wait_recv()

        cx = push(me, 2, 2, cross)
        f1 = around(me, 0)
        cx2 = push(me, 0, 2, cross)
        pass_on(me, 0, BLK)
        f2 = around(me, 2)
        yield
        cx.wait_recv()
        f3 = around(other, 2)
        arrived(f1)
        w1 = push(g.slot(m4(p - e), q), 0, 2, ahead)
        x1 = [push(near[d], 0, 2, cross) for d in sides]
        yield
        arrived(f2)
        w2 = push(g.slot(m4(p - e), q), 2, 2, ahead)
        for d in sides:
            pass_on(near[d], 0, BLK)
        cx2.wait_recv()
        pass_on(other, 0, BLK)
        w1.wait_recv()
        x2 = push(g.slot(m4(p + 2), q), 0, 2, cross)
        arrived(f3)
        w3 = push(g.slot(m4(p - e), 1 - q), 2, 2, ahead)
        yield
        w2.wait_recv()
        pass_on(g.slot(m4(p + 2), q), 0, BLK)
        for u, d in zip(x1, sides):
            u.wait_recv()
            pass_on(g.slot(m4(p - d), 1 - q), 0, BLK)
        w3.wait_recv()
        x2.wait_recv()
        pass_on(g.slot(m4(p + 2), 1 - q), 0, BLK)
        yield
        for cp in down:
            cp.wait_recv()

    def scatter(g, buf, k, h, emit, ready):
        p, q = g.p, g.q
        ra, rb, ra2, rb2, oa, ob = rsa[k][h], rsb[k][h], rsa2[k][h], rsb2[k][h], sa[k][h], sb[k][h]
        xa, yb = {}, {}
        for d in (1, 3, 2, 0):
            for f in (1, 0):
                s = g.slot(m4(p + d), 1 - q if f else q)
                ready(d, f, s)
                if f:
                    xa[d] = send(blk(buf, s, 0, 2), ra.at[pl.ds(2 * d, 2)], g.dev(p, 1 - q))
                if d:
                    yb[d, f] = send(blk(buf, s, 2, 2), rb.at[pl.ds((d - 1) * 4 + f * 2, 2)], g.dev(m4(p + d), q))
        yield
        y2 = {}
        for d in (1, 3, 2):
            xa[d].wait_recv()
            for t in range(2):
                own = buf[g.slot(m4(p + d), q) * BLK + t].astype(F32)
                oa[2 * d + t] = (own + ra[2 * d + t].astype(F32)).astype(BF16)
            y2[d] = send(oa.at[pl.ds(2 * d, 2)], ra2.at[pl.ds(2 * (d - 1), 2)], g.dev(m4(p + d), q))
        for d in (1, 3, 2):
            yb[d, 1].wait_recv()
        for t in range(2):
            tot = buf[g.slot(p, 1 - q) * BLK + 2 + t].astype(F32)
            for d in (1, 3, 2):
                tot = tot + rb[(d - 1) * 4 + 2 + t].astype(F32)
            ob[t] = tot.astype(BF16)
        x2 = send(ob, rb2, g.dev(p, 1 - q))
        yield
        xa[0].wait_recv()
        for d in (1, 3, 2):
            y2[d].wait_recv()
            yb[d, 0].wait_recv()
        for t in range(2):
            tot = buf[g.slot(p, q) * BLK + t].astype(F32) + ra[t].astype(F32)
            for d in (1, 3, 2):
                tot = tot + ra2[2 * (d - 1) + t].astype(F32)
            emit(t, tot)
        x2.wait_recv()
        for t in range(2):
            tot = buf[g.slot(p, q) * BLK + 2 + t].astype(F32)
            for d in (1, 3, 2):
                tot = tot + rb[(d - 1) * 4 + t].astype(F32)
            emit(2 + t, tot + rb2[t].astype(F32))

    def spmm(row, lo, hi, unroll, src, flip, acc=None):
        axis = 0 if flip else 1

        def body(n, acc):
            for u in range(unroll):
                k = n * unroll + u
                left = jnp.concatenate([tiles[lists[row, 2 * k]], tiles[lists[row, 2 * k + 1]]], axis=axis)
                right = jnp.concatenate([src[lists[row + 1, 2 * k]], src[lists[row + 1, 2 * k + 1]]], axis=0)
                prod = lax.dot_general(left, right, (((axis,), (0,)), ((), ())), preferred_element_type=F32)
                acc = acc * lists[row + 2, k].astype(F32) + prod
                runs[k] = acc.astype(BF16)
            return acc

        return lax.fori_loop(lo, hi, body, jnp.zeros((TILE, w), F32) if acc is None else acc)

    def collect(row, slot, dst):
        def body(t, _):
            dst[slot * BLK + t] = runs[lists[row + 3, slot * BLK + t]]
            return 0

        lax.fori_loop(0, BLK, body, 0)

    def finish(gen):
        for _ in gen:
            pass

    ag = [gather(Row, xs[h], True) for h in range(H)]
    next(ag[0])

    for cp in small:
        cp.wait()
    live_r = lax.broadcasted_iota(I32, (1, SLOTS), 1) < cnt[...]
    live_c = lax.broadcasted_iota(I32, (SLOTS, 1), 0) < cnt[...]
    idx_c = jnp.transpose(idx_r[...])
    r_r, c_r = idx_r[0:1, :], idx_r[1:2, :]
    r_c, c_c = idx_c[:, 0:1], idx_c[:, 1:2]
    lists_v[...] = jnp.zeros_like(lists_v)

    def put_lists(row, a, b, cc, nd, ns):
        t_l, s_l, k_l, e_l = pair_lists(a, b, cc, live_r, live_c, nd, ns)
        lists_v[row:row + 1, :] = t_l
        lists_v[row + 1:row + 2, :] = s_l
        lists_v[row + 2:row + 3, :] = k_l
        lists_v[row + 3:row + 4, 0:nd] = e_l

    put_lists(0, r_r, r_c, c_c, NR, NC)
    next(ag[0])
    for g in ag[1:]:
        next(g)
    next(ag[0])
    for g in ag[1:]:
        next(g)
    put_lists(4, c_r, c_c, r_c, NC, NR)
    cp = pltpu.make_async_copy(lists_v, lists, ls.at[1 + H * BLK])
    cp.start()
    runs[ZERO_RUN] = jnp.zeros((TILE, w), BF16)
    for h in range(H):
        xs[h][NC] = jnp.zeros((TILE, w), BF16)
        gs[h][NR] = jnp.zeros((TILE, w), BF16)
    next(ag[0])
    for g in ag[1:]:
        next(g)
    cp.wait()
    load_tiles.wait()

    def put_y(h):
        def emit(t, v):
            ybf[pl.ds(t * TILE, TILE), pl.ds(h * w, w)] = v.astype(BF16)
        return emit

    sc = []
    for h in range(H):
        finish(ag[h])
        turns = FPAIRS // FUNROLL
        acc = spmm(0, 0, turns - 1, FUNROLL, xs[h], False)
        if h + 1 < H:
            next(ag[h + 1])
        spmm(0, turns - 1, turns, FUNROLL, xs[h], False, acc)
        g = scatter(Col, ps[h], 0, h, put_y(h), lambda d, f, s: collect(0, s, ps[h]))
        next(g)
        sc.append(g)
    for g in sc:
        next(g)
    for g in sc:
        finish(g)

    load_grad.wait()
    wb = weight[...]
    bsum = jnp.zeros((1, 256), F32)
    for t in range(BLK):
        rows = pl.ds(t * TILE, TILE)
        pre = jnp.dot(ybf[rows, :], wb, preferred_element_type=F32) + bias[...]
        sig = 1.0 / (1.0 + jnp.exp(-pre))
        output[rows, :] = (pre * sig).astype(BF16)
        slope = sig * (1.0 + pre * (1.0 - sig))
        pg = (ograd[rows, :].astype(F32) * slope).astype(BF16)
        bsum = bsum + jnp.sum(pg.astype(F32), axis=0, keepdims=True)
        zb[rows, :] = pg
        gw = lax.dot_general(pg, wb, (((1,), (1,)), ((), ())), preferred_element_type=F32).astype(BF16)
        for h in range(H):
            gs[h][j * BLK + t] = gw[:, h * w:(h + 1) * w]
    stores = [pltpu.make_async_copy(output, output_hbm, ls.at[3 + H * BLK])]
    stores[0].start()
    agc = [gather(Col, gs[h], False) for h in range(H)]
    next(agc[0])

    dw = lax.dot_general(ybf[...], zb[...], (((0,), (0,)), ((), ())), preferred_element_type=F32)
    for k in range(16):
        dbuf[k, 0:16, :] = dw[k * 16:(k + 1) * 16, :]
        dbuf[k, 16:24, :] = jnp.broadcast_to(bsum, (8, 256))
    s0 = send(dbuf.at[pl.ds((1 - c) * 8, 8)], dsib, sibling)
    next(agc[0])
    for g in agc[1:]:
        next(g)
    next(agc[0])
    for g in agc[1:]:
        next(g)
    next(agc[0])
    for g in agc[1:]:
        next(g)
    s0.wait_recv()
    for k in range(8):
        dsum[k] = dbuf[c * 8 + k] + dsib[k]
    drs[j] = dsum[j]
    chip = y * 2 + xl

    def total(ref):
        tot = ref[0]
        for k in range(1, 8):
            tot = tot + ref[k]
        return tot

    def grad_0():
        return [send(dsum.at[lax.rem(j + d, 8)], drs.at[j], (i, lax.rem(j + d, 8))) for d in range(1, 8)]

    def grad_1(s1):
        for cp in s1:
            cp.wait_recv()
        dp[chip] = total(drs)
        return [send(dp.at[chip], dp.at[chip], (lax.rem(chip + d, 8) * 2 + c, j)) for d in range(1, 8)]

    def grad_2(s2):
        for cp in s2:
            cp.wait_recv()
        dfin[c * 8 + j] = total(dp)
        return [send(dfin.at[c * 8 + j], dfin.at[c * 8 + j], (i, lax.rem(j + d, 8))) for d in range(1, 8)]

    def grad_3(s3):
        for cp in s3:
            cp.wait_recv()
        half = dfin.at[pl.ds(c * 8, 8)]
        return send(half, half, sibling)

    def grad_4(s4):
        s4.wait_recv()
        for k in range(16):
            dw_out[k * 16:(k + 1) * 16, :] = dfin[k, 0:16, :]
        db_out[...] = dfin[0, 16:17, :]
        for a, b, n in ((dw_out, dw_hbm, 4), (db_out, db_hbm, 5)):
            stores.append(pltpu.make_async_copy(a, b, ls.at[n + H * BLK]))
            stores[-1].start()

    def put_f(h):
        def emit(t, v):
            fgrad[pl.ds(t * TILE, TILE), pl.ds(h * w, w)] = v.astype(BF16)
        return emit

    def to_sibling(h):
        cps = {}
        chips = [(d, f, m4(y + d) * 2 + (1 - xl if f else xl)) for d in (1, 3, 2, 0) for f in (1, 0)]
        for d, f, k in chips:
            collect(4, k * 2 + 1 - c, qs[h])
            cps[d, f] = send(blk(qs[h], k * 2 + 1 - c), sib[h].at[pl.ds(k * BLK, BLK)], sibling)
        for d, f, k in chips:
            collect(4, k * 2 + c, qs[h])
        return cps

    def combine(h, cp, s):
        cp.wait_recv()

        def body(t, _):
            at = s * BLK + t
            qs[h][at] = (qs[h][at].astype(F32) + sib[h][(s - c) * 2 + t].astype(F32)).astype(BF16)
            return 0

        lax.fori_loop(0, BLK, body, 0)

    back = []
    finish(agc[0])
    def row_stage(h, cps):
        g = scatter(Row, qs[h], 1, h, put_f(h), lambda d, f, s: combine(h, cps[d, f], s))
        next(g)
        back.append(g)

    turns = BPAIRS // BUNROLL
    for h in range(H):
        acc = spmm(4, 0, turns // 2, BUNROLL, gs[h], True)
        if h > 0:
            row_stage(0, cps)
            s2 = grad_1(s1)
        elif H == 1:
            s1 = grad_0()
        spmm(4, turns // 2, turns, BUNROLL, gs[h], True, acc)
        cps = to_sibling(h)
        if h + 1 < H:
            finish(agc[h + 1])
            s1 = grad_0()
    if H == 1:
        s2 = grad_1(s1)
    early = len(sent)
    row_stage(H - 1, cps)
    s3 = grad_2(s2)
    for g in back[:-1]:
        next(g)
    drain(early)
    early = len(sent)
    next(back[-1])
    s4 = grad_3(s3)
    for h in range(H - 1):
        finish(back[h])
        part = pl.ds(h * w, w)
        stores.append(pltpu.make_async_copy(fgrad.at[:, part], fgrad_hbm.at[:, part], ls.at[6 + H * BLK]))
        stores[-1].start()
    drain(early)
    early = len(sent)
    grad_4(s4)
    finish(back[-1])
    part = pl.ds((H - 1) * w, w)
    stores.append(pltpu.make_async_copy(fgrad.at[:, part], fgrad_hbm.at[:, part], ls.at[7 + H * BLK]))
    stores[-1].start()
    drain(len(sent))
    for cp in stores:
        cp.wait()


def tail(*refs):
    src, dst, mid, sem = refs[:4], refs[4:8], refs[8:12], refs[12]
    first = [pltpu.make_async_copy(src[n], mid[n], sem.at[n]) for n in range(4)]
    second = [pltpu.make_async_copy(mid[n], dst[n], sem.at[4 + n]) for n in range(4)]
    for cp in first:
        cp.start()
    for n in range(4):
        first[n].wait()
        second[n].start()
    for cp in second:
        cp.wait()


def shards(H, features, weight, bias, tile_values, tile_index, tile_count, out_grad):
    w = 256 // H
    vm = lambda *s, dt=BF16: pltpu.VMEM(s, dt)
    many = lambda n, *s: [vm(n, *s)] * H
    blkT = (TILE, w)
    two = lambda n: [many(n, *blkT) for _ in range(2)]
    index_t = tile_index[0, 0].T
    sems = 180
    scratch = [
        vm(256, 256), vm(1, 256, dt=F32), vm(2, SLOTS, dt=I32),
        vm(512, 256), vm(512, 256), vm(512, 256),
        vm(256, 256, dt=F32), vm(1, 256, dt=F32),
        vm(SLOTS, TILE, TILE),
        vm(ZERO_RUN + 1, *blkT),
        vm(8, 512, dt=I32),
        pltpu.SMEM((8, 512), I32),
        many(NC + 1, *blkT),
        many(NR, *blkT),
        many(NR + 1, *blkT),
        many(NC, *blkT),
        many(32, *blkT),
        two(8), two(12), two(6), two(2), two(8), two(2),
        vm(512, 256), vm(512, 256),
        vm(16, 24, 256, dt=F32), vm(8, 24, 256, dt=F32), vm(8, 24, 256, dt=F32), vm(8, 24, 256, dt=F32),
        vm(8, 24, 256, dt=F32), vm(16, 24, 256, dt=F32),
        pltpu.SemaphoreType.DMA((sems,)), pltpu.SemaphoreType.DMA((sems,)), pltpu.SemaphoreType.DMA((12 + H * BLK,)),
    ]
    hbm = pl.BlockSpec(memory_space=pl.ANY)
    shapes = (
        jax.ShapeDtypeStruct((512, 256), BF16),
        jax.ShapeDtypeStruct((512, 256), BF16),
        jax.ShapeDtypeStruct((256, 256), F32),
        jax.ShapeDtypeStruct((1, 256), F32),
    )
    results = pl.pallas_call(
        functools.partial(kernel, H),
        out_shape=shapes,
        in_specs=[hbm] * 5 + [pl.BlockSpec(memory_space=pltpu.VMEM), hbm],
        out_specs=(hbm,) * 4,
        scratch_shapes=scratch,
        compiler_params=pltpu.CompilerParams(collective_id=0, has_side_effects=True, vmem_limit_bytes=60 << 20),
        name="layer",
    )(features, weight, bias.reshape(1, 256), tile_values, index_t, tile_count, out_grad)
    out, fg, dw, db = pl.pallas_call(
        tail,
        out_shape=shapes,
        in_specs=[hbm] * 4,
        out_specs=(hbm,) * 4,
        scratch_shapes=[pltpu.VMEM(x.shape, x.dtype) for x in shapes] + [pltpu.SemaphoreType.DMA((8,))],
        compiler_params=pltpu.CompilerParams(vmem_limit_bytes=60 << 20),
        name="results",
    )(*results)
    return out, fg, dw, db.reshape(256)


def solution(mesh):
    return jax.shard_map(
        functools.partial(shards, 2),
        mesh=mesh,
        in_specs=(
            P(("row", "col"), None),
            P(),
            P(),
            P("row", "col", None, None, None),
            P("row", "col", None, None),
            P("row", "col"),
            P(("row", "col"), None),
        ),
        out_specs=(P(("row", "col"), None), P(("row", "col"), None), P(), P()),
        check_vma=False,
    )
```

```python
import functools

import jax
import jax.numpy as jnp
from jax import lax
from jax.experimental import pallas as pl
from jax.experimental.pallas import tpu as pltpu
from jax.sharding import PartitionSpec as P

MESH = pl.DeviceIdType.MESH
TILE = 128
BLK = 4
SLOTS = 448
NR, NC = 32, 64
FPAIRS, BPAIRS = 240, 256
ZERO_RUN = 256
FUNROLL, BUNROLL = 80, 128
F32, BF16, I32 = jnp.float32, jnp.bfloat16, jnp.int32


def pair_lists(dst_r, dst_c, src_c, live_r, live_c, nd, ns):
    t_r = lax.broadcasted_iota(I32, (SLOTS, SLOTS), 1)
    t_c = lax.broadcasted_iota(I32, (SLOTS, SLOTS), 0)
    one = lambda m: m.astype(I32)
    dlive_r = jnp.where(live_r, dst_r, nd)
    dlive_c = jnp.where(live_c, dst_c, nd)
    own_cn = dlive_c == lax.broadcasted_iota(I32, (SLOTS, nd), 1)
    own_nr = dlive_r == lax.broadcasted_iota(I32, (nd, SLOTS), 0)
    n_r = jnp.sum(one(own_cn), axis=0, keepdims=True)
    n_c = jnp.sum(one(own_nr), axis=1, keepdims=True)
    half_c = (n_c + 1) // 2
    half_r = (n_r + 1) // 2
    g_c = lax.broadcasted_iota(I32, (nd, nd), 0)
    g_r = lax.broadcasted_iota(I32, (nd, nd), 1)
    base_r = jnp.sum(jnp.where(g_c < g_r, half_c, 0), axis=0, keepdims=True)
    base_c = jnp.sum(jnp.where(g_r < g_c, half_r, 0), axis=1, keepdims=True)
    rank_c = jnp.sum(one((dlive_c == dlive_r) & (t_r < t_c)), axis=1, keepdims=True)
    pos_c = jnp.sum(jnp.where(own_cn, 2 * base_r, 0), axis=1, keepdims=True) + rank_c
    pos_c = jnp.where(live_c, pos_c, 4096)
    hit = pos_c == lax.broadcasted_iota(I32, (SLOTS, 512), 1)
    slot = lax.broadcasted_iota(I32, (SLOTS, 512), 0)
    tile_l = jnp.sum(jnp.where(hit, slot, 0), axis=0, keepdims=True)
    src_l = jnp.sum(jnp.where(hit, src_c - ns, 0), axis=0, keepdims=True) + ns
    first = (base_c == lax.broadcasted_iota(I32, (nd, 512), 1)) & (n_c > 0)
    keep_l = 1 - jnp.sum(one(first), axis=0, keepdims=True)
    end_r = jnp.where(n_r > 0, base_r + half_r - 1, ZERO_RUN)
    return tile_l, src_l, keep_l, end_r


def kernel(H, feat, weight_hbm, bias_hbm, tiles_hbm, idx_hbm, cnt, ograd_hbm,
           output_hbm, fgrad_hbm, dw_hbm, db_hbm,
           weight, bias, idx_r, ograd, output, fgrad, dw_out, db_out, tiles, runs, lists_v, lists, xs, ps, gs, qs, sib, rsa, rsb, rsa2, rsb2, sa, sb, ybf, zb,
           dbuf, dsib, dsum, drs, dp, dfin, ss, rs, ls):
    w = 256 // H
    i, j = lax.axis_index("row"), lax.axis_index("col")
    y, xl, c = i // 4, lax.rem(i // 2, 2), lax.rem(i, 2)
    xh, z = j // 4, lax.rem(j, 4)
    m4 = lambda v: lax.rem(v + 4, 4)

    class Row:
        p, q = y, xl
        slot = staticmethod(lambda p, q: (p * 2 + q) * 2 + c)
        dev = staticmethod(lambda p, q: ((p * 2 + q) * 2 + c, j))

    class Col:
        p, q = z, xh
        slot = staticmethod(lambda p, q: q * 4 + p)
        dev = staticmethod(lambda p, q: (i, q * 4 + p))

    sibling = ((y * 2 + xl) * 2 + 1 - c, j)
    peers = [lax.rem(y * 2 + xl + d, 8) * 2 + c for d in range(1, 8)] + [(y * 2 + xl) * 2 + 1 - c]
    cpeers = [lax.rem(j + d, 8) for d in range(1, 8)]

    sent, drained = [], [0]

    def send(src, dst, dev):
        n = len(sent)
        cp = pltpu.make_async_remote_copy(src_ref=src, dst_ref=dst, send_sem=ss.at[n], recv_sem=rs.at[n],
                                          device_id=dev, device_id_type=MESH)
        cp.start()
        sent.append(cp)
        return cp

    def drain(until):
        for cp in sent[drained[0]:until]:
            cp.wait_send()
        drained[0] = until

    load_tiles = pltpu.make_async_copy(tiles_hbm.at[0, 0], tiles, ls.at[0])
    load_grad = pltpu.make_async_copy(ograd_hbm, ograd, ls.at[2 + H * BLK])
    loads = []
    for h in range(H):
        for t in range(BLK):
            cp = pltpu.make_async_copy(feat.at[pl.ds(t * TILE, TILE), pl.ds(h * w, w)], xs[h].at[i * BLK + t],
                                       ls.at[1 + h * BLK + t])
            cp.start()
            loads.append(cp)

    small = []
    for n, (a, b) in enumerate(((idx_hbm, idx_r), (weight_hbm, weight), (bias_hbm, bias))):
        small.append(pltpu.make_async_copy(a, b, ls.at[8 + H * BLK + n]))
        small[-1].start()
    load_grad.start()
    load_tiles.start()
    barrier = pltpu.get_barrier_semaphore()
    for r in peers:
        pl.semaphore_signal(barrier, inc=1, device_id=(r, j), device_id_type=MESH)
    for k in cpeers:
        pl.semaphore_signal(barrier, inc=1, device_id=(i, k), device_id_type=MESH)
    pl.semaphore_wait(barrier, 15)
    for cp in loads:
        cp.wait()

    blk = lambda buf, s, lo=0, n=BLK: buf.at[pl.ds(s * BLK + lo, n)]

    def gather(g, buf, relay):
        p, q = g.p, g.q
        down = []

        def pass_on(s, lo, n):
            if relay:
                part = blk(buf, s, lo, n)
                down.append(send(part, part, sibling))

        def push(s, lo, n, dev):
            part = blk(buf, s, lo, n)
            return send(part, part, dev)

        me, other = g.slot(p, q), g.slot(p, 1 - q)
        e = 1 - 2 * c
        sides = (1, 3)
        near = {d: g.slot(m4(p - d), q) for d in sides}
        cross = g.dev(p, 1 - q)
        ahead = g.dev(m4(p + e), q)
        around = lambda s, lo: [push(s, lo, 2, g.dev(m4(p + d), q)) for d in sides]

        def arrived(copies):
            for cp in copies:
                cp.wait_recv()

        cx = push(me, 2, 2, cross)
        f1 = around(me, 0)
        cx2 = push(me, 0, 2, cross)
        pass_on(me, 0, BLK)
        f2 = around(me, 2)
        yield
        cx.wait_recv()
        f3 = around(other, 2)
        arrived(f1)
        w1 = push(g.slot(m4(p - e), q), 0, 2, ahead)
        x1 = [push(near[d], 0, 2, cross) for d in sides]
        yield
        arrived(f2)
        w2 = push(g.slot(m4(p - e), q), 2, 2, ahead)
        for d in sides:
            pass_on(near[d], 0, BLK)
        cx2.wait_recv()
        pass_on(other, 0, BLK)
        w1.wait_recv()
        x2 = push(g.slot(m4(p + 2), q), 0, 2, cross)
        arrived(f3)
        w3 = push(g.slot(m4(p - e), 1 - q), 2, 2, ahead)
        yield
        w2.wait_recv()
        pass_on(g.slot(m4(p + 2), q), 0, BLK)
        for u, d in zip(x1, sides):
            u.wait_recv()
            pass_on(g.slot(m4(p - d), 1 - q), 0, BLK)
        w3.wait_recv()
        x2.wait_recv()
        pass_on(g.slot(m4(p + 2), 1 - q), 0, BLK)
        yield
        for cp in down:
            cp.wait_recv()

    def scatter(g, buf, k, h, emit, ready):
        p, q = g.p, g.q
        ra, rb, ra2, rb2, oa, ob = rsa[k][h], rsb[k][h], rsa2[k][h], rsb2[k][h], sa[k][h], sb[k][h]
        xa, yb = {}, {}
        for d in (1, 3, 2, 0):
            for f in (1, 0):
                s = g.slot(m4(p + d), 1 - q if f else q)
                ready(d, f, s)
                if f:
                    xa[d] = send(blk(buf, s, 0, 2), ra.at[pl.ds(2 * d, 2)], g.dev(p, 1 - q))
                if d:
                    yb[d, f] = send(blk(buf, s, 2, 2), rb.at[pl.ds((d - 1) * 4 + f * 2, 2)], g.dev(m4(p + d), q))
        yield
        y2 = {}
        for d in (1, 3, 2):
            xa[d].wait_recv()
            for t in range(2):
                own = buf[g.slot(m4(p + d), q) * BLK + t].astype(F32)
                oa[2 * d + t] = (own + ra[2 * d + t].astype(F32)).astype(BF16)
            y2[d] = send(oa.at[pl.ds(2 * d, 2)], ra2.at[pl.ds(2 * (d - 1), 2)], g.dev(m4(p + d), q))
        for d in (1, 3, 2):
            yb[d, 1].wait_recv()
        for t in range(2):
            tot = buf[g.slot(p, 1 - q) * BLK + 2 + t].astype(F32)
            for d in (1, 3, 2):
                tot = tot + rb[(d - 1) * 4 + 2 + t].astype(F32)
            ob[t] = tot.astype(BF16)
        x2 = send(ob, rb2, g.dev(p, 1 - q))
        yield
        xa[0].wait_recv()
        for d in (1, 3, 2):
            y2[d].wait_recv()
            yb[d, 0].wait_recv()
        for t in range(2):
            tot = buf[g.slot(p, q) * BLK + t].astype(F32) + ra[t].astype(F32)
            for d in (1, 3, 2):
                tot = tot + ra2[2 * (d - 1) + t].astype(F32)
            emit(t, tot)
        x2.wait_recv()
        for t in range(2):
            tot = buf[g.slot(p, q) * BLK + 2 + t].astype(F32)
            for d in (1, 3, 2):
                tot = tot + rb[(d - 1) * 4 + t].astype(F32)
            emit(2 + t, tot + rb2[t].astype(F32))

    def spmm(row, lo, hi, unroll, src, flip, acc=None):
        axis = 0 if flip else 1

        def body(n, acc):
            for u in range(unroll):
                k = n * unroll + u
                left = jnp.concatenate([tiles[lists[row, 2 * k]], tiles[lists[row, 2 * k + 1]]], axis=axis)
                right = jnp.concatenate([src[lists[row + 1, 2 * k]], src[lists[row + 1, 2 * k + 1]]], axis=0)
                prod = lax.dot_general(left, right, (((axis,), (0,)), ((), ())), preferred_element_type=F32)
                acc = acc * lists[row + 2, k].astype(F32) + prod
                runs[k] = acc.astype(BF16)
            return acc

        return lax.fori_loop(lo, hi, body, jnp.zeros((TILE, w), F32) if acc is None else acc)

    def collect(row, slot, dst):
        def body(t, _):
            dst[slot * BLK + t] = runs[lists[row + 3, slot * BLK + t]]
            return 0

        lax.fori_loop(0, BLK, body, 0)

    def finish(gen):
        for _ in gen:
            pass

    ag = [gather(Row, xs[h], True) for h in range(H)]
    next(ag[0])

    for cp in small:
        cp.wait()
    live_r = lax.broadcasted_iota(I32, (1, SLOTS), 1) < cnt[...]
    live_c = lax.broadcasted_iota(I32, (SLOTS, 1), 0) < cnt[...]
    idx_c = jnp.transpose(idx_r[...])
    r_r, c_r = idx_r[0:1, :], idx_r[1:2, :]
    r_c, c_c = idx_c[:, 0:1], idx_c[:, 1:2]
    lists_v[...] = jnp.zeros_like(lists_v)

    def put_lists(row, a, b, cc, nd, ns):
        t_l, s_l, k_l, e_l = pair_lists(a, b, cc, live_r, live_c, nd, ns)
        lists_v[row:row + 1, :] = t_l
        lists_v[row + 1:row + 2, :] = s_l
        lists_v[row + 2:row + 3, :] = k_l
        lists_v[row + 3:row + 4, 0:nd] = e_l

    put_lists(0, r_r, r_c, c_c, NR, NC)
    next(ag[0])
    for g in ag[1:]:
        next(g)
    next(ag[0])
    for g in ag[1:]:
        next(g)
    put_lists(4, c_r, c_c, r_c, NC, NR)
    cp = pltpu.make_async_copy(lists_v, lists, ls.at[1 + H * BLK])
    cp.start()
    runs[ZERO_RUN] = jnp.zeros((TILE, w), BF16)
    for h in range(H):
        xs[h][NC] = jnp.zeros((TILE, w), BF16)
        gs[h][NR] = jnp.zeros((TILE, w), BF16)
    next(ag[0])
    for g in ag[1:]:
        next(g)
    cp.wait()
    load_tiles.wait()

    def put_y(h):
        def emit(t, v):
            ybf[pl.ds(t * TILE, TILE), pl.ds(h * w, w)] = v.astype(BF16)
        return emit

    sc = []
    for h in range(H):
        finish(ag[h])
        turns = FPAIRS // FUNROLL
        acc = spmm(0, 0, turns - 1, FUNROLL, xs[h], False)
        if h + 1 < H:
            next(ag[h + 1])
        spmm(0, turns - 1, turns, FUNROLL, xs[h], False, acc)
        g = scatter(Col, ps[h], 0, h, put_y(h), lambda d, f, s: collect(0, s, ps[h]))
        next(g)
        sc.append(g)
    for g in sc:
        next(g)
    for g in sc:
        finish(g)

    load_grad.wait()
    wb = weight[...]
    bsum = jnp.zeros((1, 256), F32)
    for t in range(BLK):
        rows = pl.ds(t * TILE, TILE)
        pre = jnp.dot(ybf[rows, :], wb, preferred_element_type=F32) + bias[...]
        sig = 1.0 / (1.0 + jnp.exp(-pre))
        output[rows, :] = (pre * sig).astype(BF16)
        slope = sig * (1.0 + pre * (1.0 - sig))
        pg = (ograd[rows, :].astype(F32) * slope).astype(BF16)
        bsum = bsum + jnp.sum(pg.astype(F32), axis=0, keepdims=True)
        zb[rows, :] = pg
        gw = lax.dot_general(pg, wb, (((1,), (1,)), ((), ())), preferred_element_type=F32).astype(BF16)
        for h in range(H):
            gs[h][j * BLK + t] = gw[:, h * w:(h + 1) * w]
    stores = [pltpu.make_async_copy(output, output_hbm, ls.at[3 + H * BLK])]
    stores[0].start()
    agc = [gather(Col, gs[h], False) for h in range(H)]
    next(agc[0])

    dw = lax.dot_general(ybf[...], zb[...], (((0,), (0,)), ((), ())), preferred_element_type=F32)
    for k in range(16):
        dbuf[k, 0:16, :] = dw[k * 16:(k + 1) * 16, :]
        dbuf[k, 16:24, :] = jnp.broadcast_to(bsum, (8, 256))
    s0 = send(dbuf.at[pl.ds((1 - c) * 8, 8)], dsib, sibling)
    next(agc[0])
    for g in agc[1:]:
        next(g)
    next(agc[0])
    for g in agc[1:]:
        next(g)
    next(agc[0])
    for g in agc[1:]:
        next(g)
    s0.wait_recv()
    for k in range(8):
        dsum[k] = dbuf[c * 8 + k] + dsib[k]
    drs[j] = dsum[j]
    chip = y * 2 + xl

    def total(ref):
        tot = ref[0]
        for k in range(1, 8):
            tot = tot + ref[k]
        return tot

    def grad_0():
        return [send(dsum.at[lax.rem(j + d, 8)], drs.at[j], (i, lax.rem(j + d, 8))) for d in range(1, 8)]

    def grad_1(s1):
        for cp in s1:
            cp.wait_recv()
        dp[chip] = total(drs)
        return [send(dp.at[chip], dp.at[chip], (lax.rem(chip + d, 8) * 2 + c, j)) for d in range(1, 8)]

    def grad_2(s2):
        for cp in s2:
            cp.wait_recv()
        dfin[c * 8 + j] = total(dp)
        return [send(dfin.at[c * 8 + j], dfin.at[c * 8 + j], (i, lax.rem(j + d, 8))) for d in range(1, 8)]

    def grad_3(s3):
        for cp in s3:
            cp.wait_recv()
        half = dfin.at[pl.ds(c * 8, 8)]
        return send(half, half, sibling)

    def grad_4(s4):
        s4.wait_recv()
        for k in range(16):
            dw_out[k * 16:(k + 1) * 16, :] = dfin[k, 0:16, :]
        db_out[...] = dfin[0, 16:17, :]
        for a, b, n in ((dw_out, dw_hbm, 4), (db_out, db_hbm, 5)):
            stores.append(pltpu.make_async_copy(a, b, ls.at[n + H * BLK]))
            stores[-1].start()

    def put_f(h):
        def emit(t, v):
            fgrad[pl.ds(t * TILE, TILE), pl.ds(h * w, w)] = v.astype(BF16)
        return emit

    def to_sibling(h):
        cps = {}
        chips = [(d, f, m4(y + d) * 2 + (1 - xl if f else xl)) for d in (1, 3, 2, 0) for f in (1, 0)]
        for d, f, k in chips:
            collect(4, k * 2 + 1 - c, qs[h])
            cps[d, f] = send(blk(qs[h], k * 2 + 1 - c), sib[h].at[pl.ds(k * BLK, BLK)], sibling)
        for d, f, k in chips:
            collect(4, k * 2 + c, qs[h])
        return cps

    def combine(h, cp, s):
        cp.wait_recv()

        def body(t, _):
            at = s * BLK + t
            qs[h][at] = (qs[h][at].astype(F32) + sib[h][(s - c) * 2 + t].astype(F32)).astype(BF16)
            return 0

        lax.fori_loop(0, BLK, body, 0)

    back = []
    finish(agc[0])
    def row_stage(h, cps):
        g = scatter(Row, qs[h], 1, h, put_f(h), lambda d, f, s: combine(h, cps[d, f], s))
        next(g)
        back.append(g)

    turns = BPAIRS // BUNROLL
    for h in range(H):
        acc = spmm(4, 0, turns // 2, BUNROLL, gs[h], True)
        if h > 0:
            row_stage(0, cps)
            s2 = grad_1(s1)
        elif H == 1:
            s1 = grad_0()
        spmm(4, turns // 2, turns, BUNROLL, gs[h], True, acc)
        cps = to_sibling(h)
        if h + 1 < H:
            finish(agc[h + 1])
            s1 = grad_0()
    if H == 1:
        s2 = grad_1(s1)
    early = len(sent)
    row_stage(H - 1, cps)
    s3 = grad_2(s2)
    for g in back[:-1]:
        next(g)
    drain(early)
    early = len(sent)
    next(back[-1])
    s4 = grad_3(s3)
    for h in range(H - 1):
        finish(back[h])
        part = pl.ds(h * w, w)
        stores.append(pltpu.make_async_copy(fgrad.at[:, part], fgrad_hbm.at[:, part], ls.at[6 + H * BLK]))
        stores[-1].start()
    drain(early)
    early = len(sent)
    grad_4(s4)
    finish(back[-1])
    part = pl.ds((H - 1) * w, w)
    stores.append(pltpu.make_async_copy(fgrad.at[:, part], fgrad_hbm.at[:, part], ls.at[7 + H * BLK]))
    stores[-1].start()
    drain(len(sent))
    for cp in stores:
        cp.wait()


def tail(*refs):
    src, dst, mid, sem = refs[:4], refs[4:8], refs[8:12], refs[12]
    first = [pltpu.make_async_copy(src[n], mid[n], sem.at[n]) for n in range(4)]
    second = [pltpu.make_async_copy(mid[n], dst[n], sem.at[4 + n]) for n in range(4)]
    for cp in first:
        cp.start()
    for n in range(4):
        first[n].wait()
        second[n].start()
    for cp in second:
        cp.wait()


def shards(H, features, weight, bias, tile_values, tile_index, tile_count, out_grad):
    w = 256 // H
    vm = lambda *s, dt=BF16: pltpu.VMEM(s, dt)
    many = lambda n, *s: [vm(n, *s)] * H
    blkT = (TILE, w)
    two = lambda n: [many(n, *blkT) for _ in range(2)]
    index_t = tile_index[0, 0].T
    sems = 180
    scratch = [
        vm(256, 256), vm(1, 256, dt=F32), vm(2, SLOTS, dt=I32),
        vm(512, 256), vm(512, 256), vm(512, 256),
        vm(256, 256, dt=F32), vm(1, 256, dt=F32),
        vm(SLOTS, TILE, TILE),
        vm(ZERO_RUN + 1, *blkT),
        vm(8, 512, dt=I32),
        pltpu.SMEM((8, 512), I32),
        many(NC + 1, *blkT),
        many(NR, *blkT),
        many(NR + 1, *blkT),
        many(NC, *blkT),
        many(32, *blkT),
        two(8), two(12), two(6), two(2), two(8), two(2),
        vm(512, 256), vm(512, 256),
        vm(16, 24, 256, dt=F32), vm(8, 24, 256, dt=F32), vm(8, 24, 256, dt=F32), vm(8, 24, 256, dt=F32),
        vm(8, 24, 256, dt=F32), vm(16, 24, 256, dt=F32),
        pltpu.SemaphoreType.DMA((sems,)), pltpu.SemaphoreType.DMA((sems,)), pltpu.SemaphoreType.DMA((12 + H * BLK,)),
    ]
    hbm = pl.BlockSpec(memory_space=pl.ANY)
    shapes = (
        jax.ShapeDtypeStruct((512, 256), BF16),
        jax.ShapeDtypeStruct((512, 256), BF16),
        jax.ShapeDtypeStruct((256, 256), F32),
        jax.ShapeDtypeStruct((1, 256), F32),
    )
    results = pl.pallas_call(
        functools.partial(kernel, H),
        out_shape=shapes,
        in_specs=[hbm] * 5 + [pl.BlockSpec(memory_space=pltpu.VMEM), hbm],
        out_specs=(hbm,) * 4,
        scratch_shapes=scratch,
        compiler_params=pltpu.CompilerParams(collective_id=0, has_side_effects=True, vmem_limit_bytes=60 << 20),
        name="layer",
    )(features, weight, bias.reshape(1, 256), tile_values, index_t, tile_count, out_grad)
    out, fg, dw, db = pl.pallas_call(
        tail,
        out_shape=shapes,
        in_specs=[hbm] * 4,
        out_specs=(hbm,) * 4,
        scratch_shapes=[pltpu.VMEM(x.shape, x.dtype) for x in shapes] + [pltpu.SemaphoreType.DMA((8,))],
        compiler_params=pltpu.CompilerParams(vmem_limit_bytes=60 << 20),
        name="results",
    )(*results)
    return out, fg, dw, db.reshape(256)


def solution(mesh):
    return jax.shard_map(
        functools.partial(shards, 2),
        mesh=mesh,
        in_specs=(
            P(("row", "col"), None),
            P(),
            P(),
            P("row", "col", None, None, None),
            P("row", "col", None, None),
            P("row", "col"),
            P(("row", "col"), None),
        ),
        out_specs=(P(("row", "col"), None), P(("row", "col"), None), P(), P()),
        check_vma=False,
    )
```
